512 devices in a mesh: ctx: 64 (over z, y), head: 8 (over x, core).
Axes of the slice: x: 4, y: 8, z: 8, core: 2. Of those that a mesh axis runs over, the one named last changes fastest.
Arguments:
- queries: bfloat16 [32768, 4096], P(('ctx', 'head')), may hold values from -0.625 to 0.625
- keys: bfloat16 [32768, 4096], P(('ctx', 'head')), may hold values from -0.625 to 0.625
- values: bfloat16 [32768, 4096], P(('ctx', 'head')), may hold values from -0.625 to 0.625
- out_grad: bfloat16 [32768, 4096], P(('ctx', 'head')), may hold values from -0.625 to 0.625
- doc_ids: int32 [32768], replicated, may hold values from 0 to 7, as said below
Outputs:
- attended: bfloat16 [32768, 4096], P('ctx', 'head')
- grad_queries: bfloat16 [32768, 4096], P('ctx', 'head')
- grad_keys: bfloat16 [32768, 4096], P('ctx', 'head')
- grad_values: bfloat16 [32768, 4096], P('ctx', 'head')
The draws below stay inside these ranges and needn't reach their ends.
Inputs may be any that keep to these rules, and one draw needn't show every extreme that they name: `doc_ids`: document ids start at 0, never fall along the window and rise by one at each document start; all 8 documents occur, each holds 1 to 16384 tokens, one exactly 16384.
All inputs are finite; a program needn't handle non-finite values.
Results may differ from the reference program's by a relative error of at most 0.015.
Values may be sent and summed in bfloat16 or wider, within the bound.
A program may use at most 128 MiB of HBM per device.

```python
import jax
import jax.numpy as jnp
from jax import lax

HEADS = 32
DH = 128
TOK_DEV = 512
DOCS = 8
TOKENS = 32768


def draw_doc_ids(key, part):
    key = jax.random.fold_in(key, 7)
    key_cuts, key_big = jax.random.split(key)
    half = TOKENS // 2
    cuts = jnp.sort(jax.random.permutation(key_cuts, half - 1)[:DOCS - 2].astype(jnp.int32) + 1)
    bounds = jnp.concatenate([jnp.zeros((1,), jnp.int32), cuts, jnp.full((1,), half, jnp.int32)])
    lengths = bounds[1:] - bounds[:-1]
    big = jax.random.randint(key_big, (), 0, DOCS).astype(jnp.int32)
    index = jnp.arange(DOCS, dtype=jnp.int32)
    source = jnp.clip(index - (index > big).astype(jnp.int32), 0, DOCS - 2)
    sizes_all = jnp.where(index == big, jnp.int32(half), jnp.take(lengths, source))
    starts = jnp.cumsum(sizes_all) - sizes_all
    positions = jnp.arange(TOKENS, dtype=jnp.int32)
    ids = jnp.sum((positions[:, None] >= starts[None, 1:]).astype(jnp.int32), axis=1)
    return ids.astype(jnp.int32)


def steps_of(rng, extent, cuts, least, high):
    def one(position, parts):
        draws = jax.random.uniform(jax.random.fold_in(jax.random.fold_in(rng, 6), position), (parts,), jnp.float32, least / len(cuts), high / len(cuts))
        return jnp.repeat(jnp.exp(draws), extent[position] // parts).reshape((-1,) + (1,) * (len(extent) - position - 1))

    loudness = one(*cuts[0])
    for cut in cuts[1:]:
        loudness = loudness * one(*cut)
    return loudness


def centred(key, shape, deviation, reach, cuts=(), kind=jnp.bfloat16):
    result = jax.random.normal(key, shape, jnp.float32) * deviation
    if len(cuts) > 0:
        result = steps_of(key, shape, cuts, -0.22, 0.18) * result
    return jnp.clip(result, min=-reach, max=reach).astype(kind)


def setup_inputs(seed: int = 0) -> dict:
    splits = jax.random.split(jax.random.key(seed), 6)
    return {
        "queries": centred(splits[0], (TOKENS, HEADS * DH), ((DH * TOKENS // DOCS) ** -0.1667), 0.625, ((0, 512),)),
        "keys": centred(splits[1], (TOKENS, HEADS * DH), ((DH * TOKENS // DOCS) ** -0.1667), 0.625, ((0, 512),)),
        "values": centred(splits[2], (TOKENS, HEADS * DH), ((DH * TOKENS // DOCS) ** -0.1667), 0.625, ((0, 512),)),
        "out_grad": centred(splits[3], (TOKENS, HEADS * DH), ((DH * TOKENS // DOCS) ** -0.1667), 0.625, ((0, 512),)),
        "doc_ids": draw_doc_ids(jax.random.fold_in(splits[5], 71), 0),
    }


def to_blocks(array):
    return array.reshape(TOKENS // TOK_DEV, TOK_DEV, HEADS, DH).astype(jnp.float32)


def block_scores(query_blk, key_blk, value_blk, grad_blk, doc_blk):
    positions = jnp.arange(TOK_DEV)
    allowed = (positions[:, None] >= positions[None, :]) & (doc_blk[:, None] == doc_blk[None, :])
    scores = jnp.einsum('thd,shd->hts', query_blk, key_blk)
    scores = jnp.where(allowed[None], scores, 0.0).astype(jnp.bfloat16).astype(jnp.float32)
    dscores = jnp.einsum('thd,shd->hts', grad_blk, value_blk)
    dscores = jnp.where(allowed[None], dscores, 0.0).astype(jnp.bfloat16).astype(jnp.float32)
    return scores, dscores


def reference(queries, keys, values, out_grad, doc_ids):
    query_all = to_blocks(queries)
    key_all = to_blocks(keys)
    value_all = to_blocks(values)
    grad_all = to_blocks(out_grad)
    doc_all = doc_ids.reshape(TOKENS // TOK_DEV, TOK_DEV)

    def forward_block(carry, inputs):
        state, prior_doc = carry
        query_blk, key_blk, value_blk, grad_blk, doc_blk = inputs
        scores, dscores = block_scores(query_blk, key_blk, value_blk, grad_blk, doc_blk)
        match = (doc_blk == prior_doc).astype(jnp.float32)[:, None, None]
        held = state.astype(jnp.bfloat16).astype(jnp.float32)
        attended = jnp.einsum('hts,shd->thd', scores, value_blk) + match * jnp.einsum('thi,hij->thj', query_blk, held)
        grad_query = jnp.einsum('hts,shd->thd', dscores, key_blk) + match * jnp.einsum('thj,hij->thi', grad_blk, held)
        last_doc = doc_blk[-1]
        tail_mask = (doc_blk == last_doc).astype(jnp.float32)[:, None, None]
        local_state = jnp.einsum('thi,thj->hij', key_blk * tail_mask, value_blk)
        keep = (last_doc == prior_doc).astype(jnp.float32)
        return (local_state + keep * state, last_doc), (attended.astype(jnp.bfloat16), grad_query.astype(jnp.bfloat16))

    def backward_block(carry, inputs):
        gstate, next_doc = carry
        query_blk, key_blk, value_blk, grad_blk, doc_blk = inputs
        scores, dscores = block_scores(query_blk, key_blk, value_blk, grad_blk, doc_blk)
        back = (doc_blk == next_doc).astype(jnp.float32)[:, None, None]
        gheld = gstate.astype(jnp.bfloat16).astype(jnp.float32)
        grad_key = jnp.einsum('hts,thd->shd', dscores, query_blk) + back * jnp.einsum('shj,hij->shi', value_blk, gheld)
        grad_value = jnp.einsum('hts,thj->shj', scores, grad_blk) + back * jnp.einsum('shi,hij->shj', key_blk, gheld)
        first_doc = doc_blk[0]
        lead_mask = (doc_blk == first_doc).astype(jnp.float32)[:, None, None]
        local_grad = jnp.einsum('thi,thj->hij', query_blk * lead_mask, grad_blk)
        keep = (first_doc == next_doc).astype(jnp.float32)
        return (local_grad + keep * gstate, first_doc), (grad_key.astype(jnp.bfloat16), grad_value.astype(jnp.bfloat16))

    empty_state = jnp.zeros((HEADS, DH, DH), jnp.float32)
    inputs = (query_all, key_all, value_all, grad_all, doc_all)
    carried, forward_out = lax.scan(forward_block, (empty_state, jnp.int32(-1)), inputs)
    carried_back, backward_out = lax.scan(backward_block, (empty_state, jnp.int32(-1)), inputs, reverse=True)
    whole = (TOKENS, HEADS * DH)
    return (forward_out[0].reshape(whole), forward_out[1].reshape(whole),
            backward_out[0].reshape(whole), backward_out[1].reshape(whole))
```

```python
import functools

import jax
import jax.numpy as jnp
from jax import lax
from jax.experimental import pallas as pl
from jax.experimental.pallas import tpu as pltpu
from jax.sharding import PartitionSpec as P

DH = 128
ROW = 8
MESH = pl.DeviceIdType.MESH
F32, BF16 = jnp.float32, jnp.bfloat16
K, V, Q, G = range(4)


def nt(a, b):
    return lax.dot_general(a, b, (((1,), (1,)), ((), ())), preferred_element_type=F32)


def nn(a, b):
    return lax.dot_general(a, b, (((1,), (0,)), ((), ())), preferred_element_type=F32)


def tn(a, b):
    return lax.dot_general(a, b, (((0,), (0,)), ((), ())), preferred_element_type=F32)


def one_if(flag):
    return jnp.where(flag, F32(1.0), F32(0.0))


def kernel(
    nx, ny, nz, heads, tok,
    q_ref, k_ref, v_ref, g_ref, docs_ref,
    att_ref, gq_ref, gk_ref, gv_ref,
    buf, acc, allow, allow_t, cols, docs_v, docs_s,
    st, y_in, z_out, z_in, p_out, held,
    docs_sem, own_sem, a_send, a_recv, y_send, y_recv, z_send, z_recv, p_send, p_recv,
):
    ctx = lax.axis_index("ctx")
    me_x = lax.axis_index("head")
    me_z, me_y = ctx // ny, ctx % ny
    part = tok // nx
    rows = DH // ny
    per = tok // 128
    blocks = ny * nz

    def x_peer(step):
        return lax.rem(me_x + step, nx)

    def y_peer(step):
        return lax.rem(me_y + step, ny)

    def z_peer(step):
        return lax.rem(me_z + step, nz)

    docs_copies = [
        pltpu.make_async_copy(docs_ref, docs_s, docs_sem.at[0]),
        pltpu.make_async_copy(docs_ref, docs_v, docs_sem.at[1]),
    ]
    for copy in docs_copies:
        copy.start()

    barrier = pltpu.get_barrier_semaphore()
    for step in range(1, nx):
        pl.semaphore_signal(barrier, inc=1, device_id={"head": x_peer(step)}, device_id_type=MESH)
    for step in range(1, ny):
        pl.semaphore_signal(barrier, inc=1, device_id={"ctx": me_z * ny + y_peer(step)}, device_id_type=MESH)
    for step in range(1, nz):
        pl.semaphore_signal(barrier, inc=1, device_id={"ctx": z_peer(step) * ny + me_y}, device_id_type=MESH)
    pl.semaphore_wait(barrier, nx + ny + nz - 3)

    sources = (k_ref, v_ref, q_ref, g_ref)
    mine = pl.ds(pl.multiple_of(me_x * part, part), part)

    def columns(owner, h):
        return pl.ds(pl.multiple_of((owner * heads + h) * DH, DH), DH)

    def send_tokens(h, carry):
        for a in range(4):
            pltpu.make_async_copy(
                sources[a].at[:, columns(me_x, h)], buf.at[a, h, mine, :], own_sem.at[a, h]
            ).start()
            for step in range(1, nx):
                peer = x_peer(step)
                pltpu.make_async_remote_copy(
                    src_ref=sources[a].at[:, columns(peer, h)],
                    dst_ref=buf.at[a, h, mine, :],
                    send_sem=a_send.at[a, h],
                    recv_sem=a_recv.at[a, h],
                    device_id={"head": peer},
                    device_id_type=MESH,
                ).start()
        return carry

    lax.fori_loop(0, heads, send_tokens, 0)

    def wait_bytes(ref, sem):
        pltpu.make_async_copy(ref, ref, sem).wait()

    for copy in docs_copies:
        copy.wait()

    def last(block):
        return docs_s[block * per + per - 1, 127]

    def first(block):
        return docs_s[block * per, 0]

    prior_doc = jnp.where(ctx == 0, -1, last(jnp.maximum(ctx - 1, 0)))
    next_doc = jnp.where(ctx == blocks - 1, -1, first(jnp.minimum(ctx + 1, blocks - 1)))
    last_doc, first_doc = last(ctx), first(ctx)

    local = docs_v[pl.ds(pl.multiple_of(ctx * per, per), per), :]
    row_of = [jnp.broadcast_to(local[i : i + 1, :], (128, 128)) for i in range(per)]
    col_of = [r.T for r in row_of]
    t_pos = lax.broadcasted_iota(jnp.int32, (128, 128), 0)
    s_pos = lax.broadcasted_iota(jnp.int32, (128, 128), 1)
    for i in range(per):
        at = slice(i * 128, (i + 1) * 128)
        for n, doc in enumerate((last_doc, first_doc, prior_doc, next_doc)):
            cols[n, at, :] = one_if(col_of[i] == doc).astype(BF16)
        for j in range(per):
            to = slice(j * 128, (j + 1) * 128)
            same = col_of[i] == row_of[j]
            allow[at, to] = one_if(same & (t_pos + i * 128 >= s_pos + j * 128)).astype(BF16)
            allow_t[at, to] = one_if(same & (t_pos + i * 128 <= s_pos + j * 128)).astype(BF16)

    tile = min(256, tok)

    def intra(h, left, right, by_row, by_col):
        for i in range(tok // tile):
            at, upto = slice(i * tile, (i + 1) * tile), slice(0, (i + 1) * tile)
            s = nt(buf[left, h, at, :], buf[right, h, upto, :]).astype(BF16) * allow[at, upto]
            acc[by_row[0], h, at, :] = nn(s, buf[by_row[1], h, upto, :])
            onward = slice(i * tile, tok)
            s = nt(buf[right, h, at, :], buf[left, h, onward, :]).astype(BF16) * allow_t[at, onward]
            acc[by_col[0], h, at, :] = nn(s, buf[by_col[1], h, onward, :])

    def stage_states(h):
        for a in (K, V):
            wait_bytes(buf.at[a, h, pl.ds(0, part), :], own_sem.at[a, h])
            wait_bytes(buf.at[a, h, pl.ds(0, tok - part), :], a_recv.at[a, h])
        st[h, 0] = tn(buf[K, h] * cols[0], buf[V, h]).astype(BF16)
        for a in (Q, G):
            wait_bytes(buf.at[a, h, pl.ds(0, part), :], own_sem.at[a, h])
            wait_bytes(buf.at[a, h, pl.ds(0, tok - part), :], a_recv.at[a, h])
        st[h, 1] = tn(buf[Q, h] * cols[1], buf[G, h]).astype(BF16)
        for step in range(1, ny):
            peer = y_peer(step)
            pltpu.make_async_remote_copy(
                src_ref=st.at[h, :, pl.ds(pl.multiple_of(peer * rows, rows), rows), :],
                dst_ref=y_in.at[h, me_y],
                send_sem=y_send.at[h],
                recv_sem=y_recv.at[h],
                device_id={"ctx": me_z * ny + peer},
                device_id_type=MESH,
            ).start()
        y_in[h, me_y] = st[h, :, pl.ds(pl.multiple_of(me_y * rows, rows), rows), :]

    def stage_totals(h):
        wait_bytes(y_in.at[h, pl.ds(0, ny - 1)], y_recv.at[h])
        base = me_z * ny
        total = y_in[h, 0, 0].astype(F32)
        for y in range(1, ny):
            keep = one_if(last(base + y) == last(base + y - 1))
            total = y_in[h, y, 0].astype(F32) + keep * total
        z_out[h, 0] = total.astype(BF16)
        total = y_in[h, ny - 1, 1].astype(F32)
        for y in reversed(range(ny - 1)):
            keep = one_if(first(base + y) == first(base + y + 1))
            total = y_in[h, y, 1].astype(F32) + keep * total
        z_out[h, 1] = total.astype(BF16)
        for step in range(1, nz):
            pltpu.make_async_remote_copy(
                src_ref=z_out.at[h, (me_z + step) // nz],
                dst_ref=z_in.at[h, me_z],
                send_sem=z_send.at[h],
                recv_sem=z_recv.at[h],
                device_id={"ctx": z_peer(step) * ny + me_y},
                device_id_type=MESH,
            ).start()
        z_in[h, me_z] = jnp.zeros((rows, DH), BF16)

    def stage_prefix(h):
        wait_bytes(z_in.at[h, pl.ds(0, nz - 1)], z_recv.at[h])
        base = me_z * ny
        before = last(jnp.maximum(base - 1, 0))
        after = first(jnp.minimum(base + ny, blocks - 1))
        state = jnp.zeros((rows, DH), F32)
        gstate = jnp.zeros((rows, DH), F32)
        for z in range(nz):
            term = z_in[h, z].astype(F32)
            state = state + one_if((z < me_z) & (last(z * ny + ny - 1) == before)) * term
            gstate = gstate + one_if((z > me_z) & (first(z * ny) == after)) * term
        for y in range(ny):
            p_out[h, y, 0] = state.astype(BF16)
            if y < ny - 1:
                keep = one_if(last(base + y) == last(jnp.maximum(base + y - 1, 0)))
                state = y_in[h, y, 0].astype(F32) + keep * state
        for y in reversed(range(ny)):
            p_out[h, y, 1] = gstate.astype(BF16)
            if y > 0:
                keep = one_if(first(base + y) == first(jnp.minimum(base + y + 1, blocks - 1)))
                gstate = y_in[h, y, 1].astype(F32) + keep * gstate
        here = pl.ds(pl.multiple_of(me_y * rows, rows), rows)
        for step in range(1, ny):
            peer = y_peer(step)
            pltpu.make_async_remote_copy(
                src_ref=p_out.at[h, peer],
                dst_ref=held.at[h, :, here, :],
                send_sem=p_send.at[h],
                recv_sem=p_recv.at[h],
                device_id={"ctx": me_z * ny + peer},
                device_id_type=MESH,
            ).start()
        held[h, :, here, :] = p_out[h, me_y]

    def stage_finish(h):
        wait_bytes(y_in.at[h, pl.ds(0, ny - 1)], p_recv.at[h])
        to = pl.ds(pl.multiple_of(h * DH, DH), DH)
        state, gstate = held[h, 0], held[h, 1]
        att_ref[:, to] = (acc[0, h] + nn(buf[Q, h] * cols[2], state)).astype(BF16)
        gq_ref[:, to] = (acc[1, h] + nt(buf[G, h] * cols[2], state)).astype(BF16)
        gk_ref[:, to] = (acc[2, h] + nt(buf[V, h] * cols[3], gstate)).astype(BF16)
        gv_ref[:, to] = (acc[3, h] + nn(buf[K, h] * cols[3], gstate)).astype(BF16)

    def turn(h, carry):
        pl.when(h < heads)(lambda: stage_states(h))
        pl.when(h > 0)(lambda: stage_prefix(h - 1))

        @pl.when(h < heads)
        def _():
            intra(h, Q, K, (0, V), (3, G))
            stage_totals(h)

        pl.when(h > 0)(lambda: stage_finish(h - 1))
        pl.when(h < heads)(lambda: intra(h, G, V, (1, K), (2, Q)))
        return carry

    lax.fori_loop(0, heads + 1, turn, 0)

    def drain(h, carry):
        for a in range(4):
            wait_bytes(buf.at[a, h, pl.ds(0, tok - part), :], a_send.at[a, h])
        wait_bytes(y_in.at[h, pl.ds(0, ny - 1)], y_send.at[h])
        wait_bytes(z_in.at[h, pl.ds(0, nz - 1)], z_send.at[h])
        wait_bytes(y_in.at[h, pl.ds(0, ny - 1)], p_send.at[h])
        return carry

    lax.fori_loop(0, heads, drain, 0)


def shards(nx, ny, nz, queries, keys, values, out_grad, doc_ids):
    part, width = queries.shape
    tok = part * nx
    heads = width // DH // nx
    rows = DH // ny
    docs = doc_ids.reshape(-1, 128)
    dma = pltpu.SemaphoreType.DMA
    return pl.pallas_call(
        functools.partial(kernel, nx, ny, nz, heads, tok),
        out_shape=[pltpu.VMEM((tok, heads * DH), BF16)] * 4,
        in_specs=[pl.BlockSpec(memory_space=pl.ANY)] * 5,
        out_specs=[pl.BlockSpec(memory_space=pltpu.VMEM)] * 4,
        scratch_shapes=[
            pltpu.VMEM((4, heads, tok, DH), BF16),
            pltpu.VMEM((4, heads, tok, DH), F32),
            pltpu.VMEM((tok, tok), BF16),
            pltpu.VMEM((tok, tok), BF16),
            pltpu.VMEM((4, tok, DH), BF16),
            pltpu.VMEM(docs.shape, jnp.int32),
            pltpu.SMEM(docs.shape, jnp.int32),
            pltpu.VMEM((heads, 2, DH, DH), BF16),
            pltpu.VMEM((heads, ny, 2, rows, DH), BF16),
            pltpu.VMEM((heads, 2, rows, DH), BF16),
            pltpu.VMEM((heads, nz, rows, DH), BF16),
            pltpu.VMEM((heads, ny, 2, rows, DH), BF16),
            pltpu.VMEM((heads, 2, DH, DH), BF16),
            dma((2,)),
            dma((4, heads)),
            dma((4, heads)),
            dma((4, heads)),
            dma((heads,)),
            dma((heads,)),
            dma((heads,)),
            dma((heads,)),
            dma((heads,)),
            dma((heads,)),
        ],
        compiler_params=pltpu.CompilerParams(
            collective_id=0, has_side_effects=True, vmem_limit_bytes=40 * 1024 * 1024
        ),
    )(queries, keys, values, out_grad, docs)


def solution(mesh):
    nx, blocks = mesh.shape["head"], mesh.shape["ctx"]
    ny = min(ROW, blocks)
    rows = P(("ctx", "head"), None)
    return jax.shard_map(
        functools.partial(shards, nx, ny, blocks // ny),
        mesh=mesh,
        in_specs=(rows, rows, rows, rows, P()),
        out_specs=(P("ctx", "head"),) * 4,
        check_vma=False,
    )
```

```python
import functools

import jax
import jax.numpy as jnp
from jax import lax
from jax.experimental import pallas as pl
from jax.experimental.pallas import tpu as pltpu
from jax.sharding import PartitionSpec as P

DH = 128
ROW = 8
MESH = pl.DeviceIdType.MESH
F32, BF16 = jnp.float32, jnp.bfloat16
K, V, Q, G = range(4)


def nt(a, b):
    return lax.dot_general(a, b, (((1,), (1,)), ((), ())), preferred_element_type=F32)


def nn(a, b):
    return lax.dot_general(a, b, (((1,), (0,)), ((), ())), preferred_element_type=F32)


def tn(a, b):
    return lax.dot_general(a, b, (((0,), (0,)), ((), ())), preferred_element_type=F32)


def one_if(flag):
    return jnp.where(flag, F32(1.0), F32(0.0))


def kernel(
    nx, ny, nz, heads, tok,
    q_ref, k_ref, v_ref, g_ref, docs_ref,
    out_ref,
    buf, acc, allow, allow_t, cols, docs_v, docs_s,
    st, y_in, z_out, z_in, p_out, held,
    docs_sem, own_sem, a_send, a_recv, y_send, y_recv, z_send, z_recv, p_send, p_recv,
):
    ctx = lax.axis_index("ctx")
    me_x = lax.axis_index("head")
    me_z, me_y = ctx // ny, ctx % ny
    part = tok // nx
    rows = DH // ny
    per = tok // 128
    blocks = ny * nz

    def x_peer(step):
        return lax.rem(me_x + step, nx)

    def y_peer(step):
        return lax.rem(me_y + step, ny)

    def z_peer(step):
        return lax.rem(me_z + step, nz)

    docs_copies = [
        pltpu.make_async_copy(docs_ref, docs_s, docs_sem.at[0]),
        pltpu.make_async_copy(docs_ref, docs_v, docs_sem.at[1]),
    ]
    for copy in docs_copies:
        copy.start()

    barrier = pltpu.get_barrier_semaphore()
    for step in range(1, nx):
        pl.semaphore_signal(barrier, inc=1, device_id={"head": x_peer(step)}, device_id_type=MESH)
    for step in range(1, ny):
        pl.semaphore_signal(barrier, inc=1, device_id={"ctx": me_z * ny + y_peer(step)}, device_id_type=MESH)
    for step in range(1, nz):
        pl.semaphore_signal(barrier, inc=1, device_id={"ctx": z_peer(step) * ny + me_y}, device_id_type=MESH)
    pl.semaphore_wait(barrier, nx + ny + nz - 3)

    sources = (k_ref, v_ref, q_ref, g_ref)
    mine = pl.ds(pl.multiple_of(me_x * part, part), part)

    def columns(owner, h):
        return pl.ds(pl.multiple_of((owner * heads + h) * DH, DH), DH)

    def send_tokens(h, carry):
        for a in range(4):
            pltpu.make_async_copy(
                sources[a].at[:, columns(me_x, h)], buf.at[a, h, mine, :], own_sem.at[a, h]
            ).start()
            for step in range(1, nx):
                peer = x_peer(step)
                pltpu.make_async_remote_copy(
                    src_ref=sources[a].at[:, columns(peer, h)],
                    dst_ref=buf.at[a, h, mine, :],
                    send_sem=a_send.at[a, h],
                    recv_sem=a_recv.at[a, h],
                    device_id={"head": peer},
                    device_id_type=MESH,
                ).start()
        return carry

    lax.fori_loop(0, heads, send_tokens, 0)

    def wait_bytes(ref, sem):
        pltpu.make_async_copy(ref, ref, sem).wait()

    for copy in docs_copies:
        copy.wait()

    def last(block):
        return docs_s[block * per + per - 1, 127]

    def first(block):
        return docs_s[block * per, 0]

    prior_doc = jnp.where(ctx == 0, -1, last(jnp.maximum(ctx - 1, 0)))
    next_doc = jnp.where(ctx == blocks - 1, -1, first(jnp.minimum(ctx + 1, blocks - 1)))
    last_doc, first_doc = last(ctx), first(ctx)

    local = docs_v[pl.ds(pl.multiple_of(ctx * per, per), per), :]
    row_of = [jnp.broadcast_to(local[i : i + 1, :], (128, 128)) for i in range(per)]
    col_of = [r.T for r in row_of]
    t_pos = lax.broadcasted_iota(jnp.int32, (128, 128), 0)
    s_pos = lax.broadcasted_iota(jnp.int32, (128, 128), 1)
    for i in range(per):
        at = slice(i * 128, (i + 1) * 128)
        for n, doc in enumerate((last_doc, first_doc, prior_doc, next_doc)):
            cols[n, at, :] = one_if(col_of[i] == doc).astype(BF16)
        for j in range(per):
            to = slice(j * 128, (j + 1) * 128)
            same = col_of[i] == row_of[j]
            allow[at, to] = one_if(same & (t_pos + i * 128 >= s_pos + j * 128)).astype(BF16)
            allow_t[at, to] = one_if(same & (t_pos + i * 128 <= s_pos + j * 128)).astype(BF16)

    tile = min(256, tok)

    def intra(h, left, right, by_row, by_col):
        for i in range(tok // tile):
            at, upto = slice(i * tile, (i + 1) * tile), slice(0, (i + 1) * tile)
            s = nt(buf[left, h, at, :], buf[right, h, upto, :]).astype(BF16) * allow[at, upto]
            acc[by_row[0], h, at, :] = nn(s, buf[by_row[1], h, upto, :])
            onward = slice(i * tile, tok)
            s = nt(buf[right, h, at, :], buf[left, h, onward, :]).astype(BF16) * allow_t[at, onward]
            acc[by_col[0], h, at, :] = nn(s, buf[by_col[1], h, onward, :])

    def stage_states(h):
        for a in (K, V):
            wait_bytes(buf.at[a, h, pl.ds(0, part), :], own_sem.at[a, h])
            wait_bytes(buf.at[a, h, pl.ds(0, tok - part), :], a_recv.at[a, h])
        st[h, 0] = tn(buf[K, h] * cols[0], buf[V, h]).astype(BF16)
        for a in (Q, G):
            wait_bytes(buf.at[a, h, pl.ds(0, part), :], own_sem.at[a, h])
            wait_bytes(buf.at[a, h, pl.ds(0, tok - part), :], a_recv.at[a, h])
        st[h, 1] = tn(buf[Q, h] * cols[1], buf[G, h]).astype(BF16)
        for step in range(1, ny):
            peer = y_peer(step)
            pltpu.make_async_remote_copy(
                src_ref=st.at[h, :, pl.ds(pl.multiple_of(peer * rows, rows), rows), :],
                dst_ref=y_in.at[h, me_y],
                send_sem=y_send.at[h],
                recv_sem=y_recv.at[h],
                device_id={"ctx": me_z * ny + peer},
                device_id_type=MESH,
            ).start()
        y_in[h, me_y] = st[h, :, pl.ds(pl.multiple_of(me_y * rows, rows), rows), :]

    def stage_totals(h):
        wait_bytes(y_in.at[h, pl.ds(0, ny - 1)], y_recv.at[h])
        base = me_z * ny
        total = y_in[h, 0, 0].astype(F32)
        for y in range(1, ny):
            keep = one_if(last(base + y) == last(base + y - 1))
            total = y_in[h, y, 0].astype(F32) + keep * total
        z_out[h, 0] = total.astype(BF16)
        total = y_in[h, ny - 1, 1].astype(F32)
        for y in reversed(range(ny - 1)):
            keep = one_if(first(base + y) == first(base + y + 1))
            total = y_in[h, y, 1].astype(F32) + keep * total
        z_out[h, 1] = total.astype(BF16)
        for step in range(1, nz):
            pltpu.make_async_remote_copy(
                src_ref=z_out.at[h, (me_z + step) // nz],
                dst_ref=z_in.at[h, me_z],
                send_sem=z_send.at[h],
                recv_sem=z_recv.at[h],
                device_id={"ctx": z_peer(step) * ny + me_y},
                device_id_type=MESH,
            ).start()
        z_in[h, me_z] = jnp.zeros((rows, DH), BF16)

    def stage_prefix(h):
        wait_bytes(z_in.at[h, pl.ds(0, nz - 1)], z_recv.at[h])
        base = me_z * ny
        before = last(jnp.maximum(base - 1, 0))
        after = first(jnp.minimum(base + ny, blocks - 1))
        state = jnp.zeros((rows, DH), F32)
        gstate = jnp.zeros((rows, DH), F32)
        for z in range(nz):
            term = z_in[h, z].astype(F32)
            state = state + one_if((z < me_z) & (last(z * ny + ny - 1) == before)) * term
            gstate = gstate + one_if((z > me_z) & (first(z * ny) == after)) * term
        for y in range(ny):
            p_out[h, y, 0] = state.astype(BF16)
            if y < ny - 1:
                keep = one_if(last(base + y) == last(jnp.maximum(base + y - 1, 0)))
                state = y_in[h, y, 0].astype(F32) + keep * state
        for y in reversed(range(ny)):
            p_out[h, y, 1] = gstate.astype(BF16)
            if y > 0:
                keep = one_if(first(base + y) == first(jnp.minimum(base + y + 1, blocks - 1)))
                gstate = y_in[h, y, 1].astype(F32) + keep * gstate
        here = pl.ds(pl.multiple_of(me_y * rows, rows), rows)
        for step in range(1, ny):
            peer = y_peer(step)
            pltpu.make_async_remote_copy(
                src_ref=p_out.at[h, peer],
                dst_ref=held.at[h, :, here, :],
                send_sem=p_send.at[h],
                recv_sem=p_recv.at[h],
                device_id={"ctx": me_z * ny + peer},
                device_id_type=MESH,
            ).start()
        held[h, :, here, :] = p_out[h, me_y]

    def stage_finish(h):
        wait_bytes(y_in.at[h, pl.ds(0, ny - 1)], p_recv.at[h])
        to = pl.ds(pl.multiple_of(h * DH, DH), DH)
        state, gstate = held[h, 0], held[h, 1]
        out_ref[0, :, to] = (acc[0, h] + nn(buf[Q, h] * cols[2], state)).astype(BF16)
        out_ref[1, :, to] = (acc[1, h] + nt(buf[G, h] * cols[2], state)).astype(BF16)
        out_ref[2, :, to] = (acc[2, h] + nt(buf[V, h] * cols[3], gstate)).astype(BF16)
        out_ref[3, :, to] = (acc[3, h] + nn(buf[K, h] * cols[3], gstate)).astype(BF16)

    def turn(t, carry):
        @pl.when(t < heads)
        def _():
            stage_states(t)
            intra(t, Q, K, (0, V), (3, G))
            intra(t, G, V, (1, K), (2, Q))

        pl.when(t > 1)(lambda: stage_finish(t - 2))
        pl.when((t > 0) & (t <= heads))(lambda: stage_prefix(t - 1))
        pl.when(t < heads)(lambda: stage_totals(t))
        return carry

    lax.fori_loop(0, heads + 2, turn, 0)

    def drain(h, carry):
        for a in range(4):
            wait_bytes(buf.at[a, h, pl.ds(0, tok - part), :], a_send.at[a, h])
        wait_bytes(y_in.at[h, pl.ds(0, ny - 1)], y_send.at[h])
        wait_bytes(z_in.at[h, pl.ds(0, nz - 1)], z_send.at[h])
        wait_bytes(y_in.at[h, pl.ds(0, ny - 1)], p_send.at[h])
        return carry

    lax.fori_loop(0, heads, drain, 0)


def write_out(*refs):
    sems = refs[8]
    copies = [pltpu.make_async_copy(refs[i], refs[i + 4], sems.at[i]) for i in range(4)]
    for copy in copies:
        copy.start()
    for copy in copies:
        copy.wait()


def shards(nx, ny, nz, queries, keys, values, out_grad, doc_ids):
    part, width = queries.shape
    tok = part * nx
    heads = width // DH // nx
    rows = DH // ny
    docs = doc_ids.reshape(-1, 128)
    queries, keys, values, out_grad, docs = (
        pltpu.with_memory_space_constraint(x, pltpu.HBM)
        for x in (queries, keys, values, out_grad, docs)
    )
    dma = pltpu.SemaphoreType.DMA
    results = pl.pallas_call(
        functools.partial(kernel, nx, ny, nz, heads, tok),
        out_shape=pltpu.VMEM((4, tok, heads * DH), BF16),
        in_specs=[pl.BlockSpec(memory_space=pltpu.HBM)] * 5,
        out_specs=pl.BlockSpec(memory_space=pltpu.VMEM),
        scratch_shapes=[
            pltpu.VMEM((4, heads, tok, DH), BF16),
            pltpu.VMEM((4, heads, tok, DH), F32),
            pltpu.VMEM((tok, tok), BF16),
            pltpu.VMEM((tok, tok), BF16),
            pltpu.VMEM((4, tok, DH), BF16),
            pltpu.VMEM(docs.shape, jnp.int32),
            pltpu.SMEM(docs.shape, jnp.int32),
            pltpu.VMEM((heads, 2, DH, DH), BF16),
            pltpu.VMEM((heads, ny, 2, rows, DH), BF16),
            pltpu.VMEM((heads, 2, rows, DH), BF16),
            pltpu.VMEM((heads, nz, rows, DH), BF16),
            pltpu.VMEM((heads, ny, 2, rows, DH), BF16),
            pltpu.VMEM((heads, 2, DH, DH), BF16),
            dma((2,)),
            dma((4, heads)),
            dma((4, heads)),
            dma((4, heads)),
            dma((heads,)),
            dma((heads,)),
            dma((heads,)),
            dma((heads,)),
            dma((heads,)),
            dma((heads,)),
        ],
        compiler_params=pltpu.CompilerParams(
            collective_id=0, has_side_effects=True, vmem_limit_bytes=40 * 1024 * 1024
        ),
    )(queries, keys, values, out_grad, docs)
    return tuple(results[i] for i in range(4))


def solution(mesh):
    nx, blocks = mesh.shape["head"], mesh.shape["ctx"]
    ny = min(ROW, blocks)
    rows = P(("ctx", "head"), None)
    return jax.shard_map(
        functools.partial(shards, nx, ny, blocks // ny),
        mesh=mesh,
        in_specs=(rows, rows, rows, rows, P()),
        out_specs=(P("ctx", "head"),) * 4,
        check_vma=False,
    )
```

```python
import functools

import jax
import jax.numpy as jnp
from jax import lax
from jax.experimental import pallas as pl
from jax.experimental.pallas import tpu as pltpu
from jax.sharding import PartitionSpec as P

DH = 128
ROW = 8
GROUP = 1
MESH = pl.DeviceIdType.MESH
F32, BF16 = jnp.float32, jnp.bfloat16
K, V, Q, G = range(4)


def nt(a, b):
    return lax.dot_general(a, b, (((1,), (1,)), ((), ())), preferred_element_type=F32)


def nn(a, b):
    return lax.dot_general(a, b, (((1,), (0,)), ((), ())), preferred_element_type=F32)


def tn(a, b):
    return lax.dot_general(a, b, (((0,), (0,)), ((), ())), preferred_element_type=F32)


def one_if(flag):
    return jnp.where(flag, F32(1.0), F32(0.0))


def wait_bytes(ref, sem):
    pltpu.make_async_copy(ref, ref, sem).wait()


def kernel(
    nx, ny, nz, heads, tok, group,
    q_ref, k_ref, v_ref, g_ref, docs_ref,
    out_ref,
    pair, buf, acc, allow, allow_t, cols, docs_v, docs_s, keeps,
    part_out, part_in, st, y_in, z_out, z_in, p_out, held,
    docs_sem, own_sem, pair_send, pair_recv, part_send, part_recv,
    mine_sem, tok_send, tok_recv, y_send, y_recv, z_send, z_recv, p_send, p_recv,
):
    ctx = lax.axis_index("ctx")
    me_x = lax.axis_index("head")
    me_z, me_y = ctx // ny, ctx % ny
    chip, core = me_x // 2, me_x % 2
    chips = nx // 2
    groups = heads // group
    part = tok // nx
    both = 2 * part
    rows = DH // ny
    per = tok // 128
    blocks = ny * nz
    wide = group * DH

    def at_chip(step):
        return {"head": lax.rem(chip + step, chips) * 2 + core}

    def y_peer(step):
        return lax.rem(me_y + step, ny)

    def at_y(step):
        return {"ctx": me_z * ny + y_peer(step)}

    def at_z(step):
        return {"ctx": lax.rem(me_z + step, nz) * ny + me_y}

    sibling = {"head": me_x + 1 - 2 * core}
    sources = (k_ref, v_ref, q_ref, g_ref)
    own_rows = pl.ds(pl.multiple_of(core * part, part), part)

    def columns(owner, first):
        return pl.ds(pl.multiple_of((owner * heads + first) * DH, DH), wide)

    docs_copies = [
        pltpu.make_async_copy(docs_ref, docs_s, docs_sem.at[0]),
        pltpu.make_async_copy(docs_ref, docs_v, docs_sem.at[1]),
    ]
    for copy in docs_copies:
        copy.start()
    for g in range(groups):
        for a in range(4):
            for c in range(chips):
                pltpu.make_async_copy(
                    sources[a].at[:, columns(c * 2 + core, g * group)],
                    pair.at[a, c, own_rows, pl.ds(g * wide, wide)],
                    own_sem.at[g],
                ).start()

    barrier = pltpu.get_barrier_semaphore()
    peers = [sibling]
    peers += [at_chip(step) for step in range(1, chips)]
    peers += [at_y(step) for step in range(1, ny)]
    peers += [at_z(step) for step in range(1, nz)]
    for peer in peers:
        pl.semaphore_signal(barrier, inc=1, device_id=peer, device_id_type=MESH)
    pl.semaphore_wait(barrier, len(peers))

    for g in range(groups):
        for a in range(4):
            for c in range(chips):
                pltpu.make_async_remote_copy(
                    src_ref=sources[a].at[:, columns(c * 2 + 1 - core, g * group)],
                    dst_ref=pair.at[a, c, own_rows, pl.ds(g * wide, wide)],
                    send_sem=pair_send.at[g],
                    recv_sem=pair_recv.at[g],
                    device_id=sibling,
                    device_id_type=MESH,
                ).start()

    for copy in docs_copies:
        copy.wait()

    def last(block):
        return docs_s[block * per + per - 1, 127]

    def first(block):
        return docs_s[block * per, 0]

    prior_doc = jnp.where(ctx == 0, -1, last(jnp.maximum(ctx - 1, 0)))
    next_doc = jnp.where(ctx == blocks - 1, -1, first(jnp.minimum(ctx + 1, blocks - 1)))
    last_doc, first_doc = last(ctx), first(ctx)

    local = docs_v[pl.ds(pl.multiple_of(ctx * per, per), per), :]
    row_of = [jnp.broadcast_to(local[i : i + 1, :], (128, 128)) for i in range(per)]
    col_of = [r.T for r in row_of]
    for i in range(per):
        at = slice(i * 128, (i + 1) * 128)
        for n, doc in enumerate((last_doc, first_doc, prior_doc, next_doc)):
            cols[n, at, :] = one_if(col_of[i] == doc).astype(BF16)

    chip_rows = pl.ds(pl.multiple_of(chip * both, both), both)

    def send_partials(g):
        half = pair.at[:, :, pl.ds(0, part), pl.ds(0, wide)]
        wait_bytes(half, own_sem.at[g])
        wait_bytes(half, pair_recv.at[g])
        tail, lead = cols[0, chip_rows, :], cols[1, chip_rows, :]
        for c in range(chips):
            for i in range(group):
                at = pl.ds((g * group + i) * DH, DH)
                part_out[g, c, i, 0] = tn(pair[K, c, :, at] * tail, pair[V, c, :, at]).astype(BF16)
                part_out[g, c, i, 1] = tn(pair[Q, c, :, at] * lead, pair[G, c, :, at]).astype(BF16)
        for step in range(1, chips):
            pltpu.make_async_remote_copy(
                src_ref=part_out.at[g, lax.rem(chip + step, chips)],
                dst_ref=part_in.at[g, chip],
                send_sem=part_send.at[g],
                recv_sem=part_recv.at[g],
                device_id=at_chip(step),
                device_id_type=MESH,
            ).start()
        part_in[g, chip] = part_out[g, chip]

    for g in range(groups):
        send_partials(g)

    def send_tokens(h, carry):
        at = pl.ds(pl.multiple_of(h * DH, DH), DH)
        for a in range(4):
            for step in range(1, chips):
                pltpu.make_async_remote_copy(
                    src_ref=pair.at[a, lax.rem(chip + step, chips), :, at],
                    dst_ref=buf.at[a, chip_rows, at],
                    send_sem=tok_send.at[h],
                    recv_sem=tok_recv.at[h],
                    device_id=at_chip(step),
                    device_id_type=MESH,
                ).start()
            pltpu.make_async_copy(
                pair.at[a, chip, :, at], buf.at[a, chip_rows, at], mine_sem.at[h]
            ).start()
        return carry

    lax.fori_loop(0, heads, send_tokens, 0)

    t_pos = lax.broadcasted_iota(jnp.int32, (128, 128), 0)
    s_pos = lax.broadcasted_iota(jnp.int32, (128, 128), 1)
    for i in range(per):
        at = slice(i * 128, (i + 1) * 128)
        for j in range(per):
            to = slice(j * 128, (j + 1) * 128)
            same = col_of[i] == row_of[j]
            allow[at, to] = one_if(same & (t_pos + i * 128 >= s_pos + j * 128)).astype(BF16)
            allow_t[at, to] = one_if(same & (t_pos + i * 128 <= s_pos + j * 128)).astype(BF16)

    base = me_z * ny
    before, after = last(jnp.maximum(base - 1, 0)), first(jnp.minimum(base + ny, blocks - 1))
    for y in range(ny):
        at = base + y
        keeps[0, y] = one_if(last(at) == last(jnp.maximum(at - 1, 0)))
        keeps[1, y] = one_if(first(at) == first(jnp.minimum(at + 1, blocks - 1)))
    for z in range(nz):
        keeps[2, z] = one_if((z < me_z) & (last(z * ny + ny - 1) == before))
        keeps[3, z] = one_if((z > me_z) & (first(z * ny) == after))

    def stage_states(g):
        wait_bytes(part_in.at[g, pl.ds(0, chips - 1)], part_recv.at[g])
        for i in range(group):
            for n in range(2):
                total = part_in[g, 0, i, n].astype(F32)
                for c in range(1, chips):
                    total = total + part_in[g, c, i, n].astype(F32)
                st[g, i, n] = total.astype(BF16)
        for step in range(1, ny):
            slot = pl.multiple_of(y_peer(step) * rows, rows)
            pltpu.make_async_remote_copy(
                src_ref=st.at[g, :, :, pl.ds(slot, rows), :],
                dst_ref=y_in.at[g, me_y],
                send_sem=y_send.at[g],
                recv_sem=y_recv.at[g],
                device_id=at_y(step),
                device_id_type=MESH,
            ).start()
        y_in[g, me_y] = st[g, :, :, pl.ds(pl.multiple_of(me_y * rows, rows), rows), :]

    def stage_totals(g):
        wait_bytes(y_in.at[g, pl.ds(0, ny - 1)], y_recv.at[g])
        total = y_in[g, 0, :, 0].astype(F32)
        for y in range(1, ny):
            total = y_in[g, y, :, 0].astype(F32) + keeps[0, y] * total
        z_out[g, 0] = total.astype(BF16)
        total = y_in[g, ny - 1, :, 1].astype(F32)
        for y in reversed(range(ny - 1)):
            total = y_in[g, y, :, 1].astype(F32) + keeps[1, y] * total
        z_out[g, 1] = total.astype(BF16)
        for step in range(1, nz):
            pltpu.make_async_remote_copy(
                src_ref=z_out.at[g, (me_z + step) // nz],
                dst_ref=z_in.at[g, me_z],
                send_sem=z_send.at[g],
                recv_sem=z_recv.at[g],
                device_id=at_z(step),
                device_id_type=MESH,
            ).start()
        z_in[g, me_z] = jnp.zeros((group, rows, DH), BF16)

    def stage_prefix(g):
        wait_bytes(z_in.at[g, pl.ds(0, nz - 1)], z_recv.at[g])
        state = jnp.zeros((group, rows, DH), F32)
        gstate = jnp.zeros((group, rows, DH), F32)
        for z in range(nz):
            term = z_in[g, z].astype(F32)
            state = state + keeps[2, z] * term
            gstate = gstate + keeps[3, z] * term
        for y in range(ny):
            p_out[g, y, :, 0] = state.astype(BF16)
            if y < ny - 1:
                state = y_in[g, y, :, 0].astype(F32) + keeps[0, y] * state
        for y in reversed(range(ny)):
            p_out[g, y, :, 1] = gstate.astype(BF16)
            if y > 0:
                gstate = y_in[g, y, :, 1].astype(F32) + keeps[1, y] * gstate
        here = pl.ds(pl.multiple_of(me_y * rows, rows), rows)
        for step in range(1, ny):
            pltpu.make_async_remote_copy(
                src_ref=p_out.at[g, y_peer(step)],
                dst_ref=held.at[g, :, :, here, :],
                send_sem=p_send.at[g],
                recv_sem=p_recv.at[g],
                device_id=at_y(step),
                device_id_type=MESH,
            ).start()
        held[g, :, :, here, :] = p_out[g, me_y]

    arrival, phase = 3.0 * group, 5.5
    stages = [(g * arrival + n * phase, n, g) for g in range(groups) for n in range(3)]
    for _, n, g in sorted(stages):
        (stage_states, stage_totals, stage_prefix)[n](g)

    tile = min(256, tok)

    def scores(h, left, right, by_row, by_col):
        here = pl.ds(pl.multiple_of(h * DH, DH), DH)
        for i in range(tok // tile):
            at, upto = slice(i * tile, (i + 1) * tile), slice(0, (i + 1) * tile)
            s = nt(buf[left, at, here], buf[right, upto, here]).astype(BF16) * allow[at, upto]
            acc[by_row[0], h, at, :] = nn(s, buf[by_row[1], upto, here])
            onward = slice(i * tile, tok)
            s = nt(buf[right, at, here], buf[left, onward, here]).astype(BF16) * allow_t[at, onward]
            acc[by_col[0], h, at, :] = nn(s, buf[by_col[1], onward, here])

    def intra(h, carry):
        wait_bytes(buf.at[:, pl.ds(0, both), pl.ds(0, DH)], mine_sem.at[h])
        wait_bytes(buf.at[:, pl.ds(0, tok - both), pl.ds(0, DH)], tok_recv.at[h])
        scores(h, Q, K, (0, V), (3, G))
        scores(h, G, V, (1, K), (2, Q))
        return carry

    def finish(h, carry):
        g, i = h // group, h % group
        here = pl.ds(pl.multiple_of(h * DH, DH), DH)
        state, gstate = held[g, i, 0], held[g, i, 1]
        match, back = cols[2], cols[3]
        out_ref[0, :, here] = (acc[0, h] + nn(buf[Q, :, here] * match, state)).astype(BF16)
        out_ref[1, :, here] = (acc[1, h] + nt(buf[G, :, here] * match, state)).astype(BF16)
        out_ref[2, :, here] = (acc[2, h] + nt(buf[V, :, here] * back, gstate)).astype(BF16)
        out_ref[3, :, here] = (acc[3, h] + nn(buf[K, :, here] * back, gstate)).astype(BF16)
        return carry

    ahead = heads - group
    lax.fori_loop(0, heads - 1, intra, 0)
    for g in range(groups - 1):
        wait_bytes(y_in.at[g, pl.ds(0, ny - 1)], p_recv.at[g])
    lax.fori_loop(0, ahead, finish, 0)
    lax.fori_loop(heads - 1, heads, intra, 0)
    wait_bytes(y_in.at[groups - 1, pl.ds(0, ny - 1)], p_recv.at[groups - 1])
    lax.fori_loop(ahead, heads, finish, 0)

    for g in range(groups):
        wait_bytes(pair.at[:, :, pl.ds(0, part), pl.ds(0, wide)], pair_send.at[g])
        wait_bytes(part_in.at[g, pl.ds(0, chips - 1)], part_send.at[g])
        wait_bytes(y_in.at[g, pl.ds(0, ny - 1)], y_send.at[g])
        wait_bytes(z_in.at[g, pl.ds(0, nz - 1)], z_send.at[g])
        wait_bytes(y_in.at[g, pl.ds(0, ny - 1)], p_send.at[g])
    for h in range(heads):
        wait_bytes(buf.at[:, pl.ds(0, tok - both), pl.ds(0, DH)], tok_send.at[h])


def shards(nx, ny, nz, queries, keys, values, out_grad, doc_ids):
    part, width = queries.shape
    tok = part * nx
    heads = width // DH // nx
    group = min(GROUP, heads)
    groups = heads // group
    chips = nx // 2
    rows = DH // ny
    docs = doc_ids.reshape(-1, 128)
    operands = [
        pltpu.with_memory_space_constraint(x, pltpu.HBM)
        for x in (queries, keys, values, out_grad, docs)
    ]
    dma = pltpu.SemaphoreType.DMA
    results = pl.pallas_call(
        functools.partial(kernel, nx, ny, nz, heads, tok, group),
        out_shape=pltpu.VMEM((4, tok, heads * DH), BF16),
        in_specs=[pl.BlockSpec(memory_space=pltpu.HBM)] * 5,
        out_specs=pl.BlockSpec(memory_space=pltpu.VMEM),
        scratch_shapes=[
            pltpu.VMEM((4, chips, 2 * part, heads * DH), BF16),
            pltpu.VMEM((4, tok, heads * DH), BF16),
            pltpu.VMEM((4, heads, tok, DH), F32),
            pltpu.VMEM((tok, tok), BF16),
            pltpu.VMEM((tok, tok), BF16),
            pltpu.VMEM((4, tok, DH), BF16),
            pltpu.VMEM(docs.shape, jnp.int32),
            pltpu.SMEM(docs.shape, jnp.int32),
            pltpu.SMEM((4, max(ny, nz)), F32),
            pltpu.VMEM((groups, chips, group, 2, DH, DH), BF16),
            pltpu.VMEM((groups, chips, group, 2, DH, DH), BF16),
            pltpu.VMEM((groups, group, 2, DH, DH), BF16),
            pltpu.VMEM((groups, ny, group, 2, rows, DH), BF16),
            pltpu.VMEM((groups, 2, group, rows, DH), BF16),
            pltpu.VMEM((groups, nz, group, rows, DH), BF16),
            pltpu.VMEM((groups, ny, group, 2, rows, DH), BF16),
            pltpu.VMEM((groups, group, 2, DH, DH), BF16),
            dma((2,)),
            dma((groups,)),
            dma((groups,)),
            dma((groups,)),
            dma((groups,)),
            dma((groups,)),
            dma((heads,)),
            dma((heads,)),
            dma((heads,)),
            dma((groups,)),
            dma((groups,)),
            dma((groups,)),
            dma((groups,)),
            dma((groups,)),
            dma((groups,)),
        ],
        compiler_params=pltpu.CompilerParams(
            collective_id=0, has_side_effects=True, vmem_limit_bytes=40 * 1024 * 1024
        ),
    )(*operands)
    return tuple(results[i] for i in range(4))


def solution(mesh):
    nx, blocks = mesh.shape["head"], mesh.shape["ctx"]
    ny = min(ROW, blocks)
    rows = P(("ctx", "head"), None)
    return jax.shard_map(
        functools.partial(shards, nx, ny, blocks // ny),
        mesh=mesh,
        in_specs=(rows, rows, rows, rows, P()),
        out_specs=(P("ctx", "head"),) * 4,
        check_vma=False,
    )
```

```python
import functools

import jax
import jax.numpy as jnp
from jax import lax
from jax.experimental import pallas as pl
from jax.experimental.pallas import tpu as pltpu
from jax.sharding import PartitionSpec as P

DH = 128
ROW = 8
GROUP = 1
MESH = pl.DeviceIdType.MESH
F32, BF16 = jnp.float32, jnp.bfloat16
K, V, Q, G = range(4)
EARLY = (K,)


def nt(a, b):
    return lax.dot_general(a, b, (((1,), (1,)), ((), ())), preferred_element_type=F32)


def nn(a, b):
    return lax.dot_general(a, b, (((1,), (0,)), ((), ())), preferred_element_type=F32)


def tn(a, b):
    return lax.dot_general(a, b, (((0,), (0,)), ((), ())), preferred_element_type=F32)


def one_if(flag):
    return jnp.where(flag, F32(1.0), F32(0.0))


def wait_bytes(ref, sem):
    pltpu.make_async_copy(ref, ref, sem).wait()


def kernel(
    nx, ny, nz, heads, tok, group,
    q_ref, k_ref, v_ref, g_ref, docs_ref,
    out_ref,
    pair, buf, acc, allow, allow_t, cols, docs_v, docs_s, keeps,
    part_out, part_in, st, y_in, z_out, z_in, p_out, held,
    docs_sem, own_sem, pair_send, pair_recv, part_send, part_recv,
    line_in, cross_in, mine_sem, tok_send, tok_recv, y_send, y_recv, z_send, z_recv, p_send, p_recv,
):
    ctx = lax.axis_index("ctx")
    me_x = lax.axis_index("head")
    me_z, me_y = ctx // ny, ctx % ny
    chip, core = me_x // 2, me_x % 2
    chips = nx // 2
    groups = heads // group
    part = tok // nx
    both = 2 * part
    rows = DH // ny
    per = tok // 128
    blocks = ny * nz
    wide = group * DH

    def at_chip(step):
        return {"head": lax.rem(chip + step, chips) * 2 + core}

    def y_peer(step):
        return lax.rem(me_y + step, ny)

    def at_y(step):
        return {"ctx": me_z * ny + y_peer(step)}

    def at_z(step):
        return {"ctx": lax.rem(me_z + step, nz) * ny + me_y}

    sibling = {"head": me_x + 1 - 2 * core}
    sources = (k_ref, v_ref, q_ref, g_ref)
    own_rows = pl.ds(pl.multiple_of(core * part, part), part)

    def columns(owner, first):
        return pl.ds(pl.multiple_of((owner * heads + first) * DH, DH), wide)

    docs_copies = [
        pltpu.make_async_copy(docs_ref, docs_s, docs_sem.at[0]),
        pltpu.make_async_copy(docs_ref, docs_v, docs_sem.at[1]),
    ]
    for copy in docs_copies:
        copy.start()
    for g in range(groups):
        for a in range(4):
            for c in range(chips):
                pltpu.make_async_copy(
                    sources[a].at[:, columns(c * 2 + core, g * group)],
                    pair.at[a, c, own_rows, pl.ds(g * wide, wide)],
                    own_sem.at[g],
                ).start()

    barrier = pltpu.get_barrier_semaphore()

    def greet(sem, peer):
        pl.semaphore_signal(sem, inc=1, device_id=peer, device_id_type=MESH)

    for step in range(1, chips):
        greet(barrier, {"head": lax.rem(chip + step, chips) * 2})
    pl.when(core == 1)(lambda: greet(barrier, sibling))
    across = [at_y(step) for step in range(1, ny)] + [at_z(step) for step in range(1, nz)]
    for peer in across:
        greet(barrier, {**peer, "head": chip * 2 + 1})

    @pl.when(core == 0)
    def _():
        pl.semaphore_wait(barrier, nx - 1)
        greet(line_in, sibling)

    @pl.when(core == 1)
    def _():
        pl.semaphore_wait(line_in, 1)

    for g in range(groups):
        for a in range(4):
            for c in range(chips):
                pltpu.make_async_remote_copy(
                    src_ref=sources[a].at[:, columns(c * 2 + 1 - core, g * group)],
                    dst_ref=pair.at[a, c, own_rows, pl.ds(g * wide, wide)],
                    send_sem=pair_send.at[g],
                    recv_sem=pair_recv.at[g],
                    device_id=sibling,
                    device_id_type=MESH,
                ).start()

    chip_rows = pl.ds(pl.multiple_of(chip * both, both), both)
    mine = pl.ds(pl.multiple_of(me_x * part, part), part)
    for a in EARLY:
        for step in range(1, chips):
            there = lax.rem(chip + step, chips) * 2
            for c in range(2):
                pltpu.make_async_remote_copy(
                    src_ref=sources[a].at[:, pl.ds(pl.multiple_of((there + c) * heads * DH, DH), DH)],
                    dst_ref=buf.at[a, mine, pl.ds(0, DH)],
                    send_sem=tok_send.at[0],
                    recv_sem=tok_recv.at[0],
                    device_id={"head": there + c},
                    device_id_type=MESH,
                ).start()

    for copy in docs_copies:
        copy.wait()

    def last(block):
        return docs_s[block * per + per - 1, 127]

    def first(block):
        return docs_s[block * per, 0]

    prior_doc = jnp.where(ctx == 0, -1, last(jnp.maximum(ctx - 1, 0)))
    next_doc = jnp.where(ctx == blocks - 1, -1, first(jnp.minimum(ctx + 1, blocks - 1)))
    last_doc, first_doc = last(ctx), first(ctx)

    local = docs_v[pl.ds(pl.multiple_of(ctx * per, per), per), :]
    row_of = [jnp.broadcast_to(local[i : i + 1, :], (128, 128)) for i in range(per)]
    col_of = [r.T for r in row_of]
    for i in range(per):
        at = slice(i * 128, (i + 1) * 128)
        for n, doc in enumerate((last_doc, first_doc, prior_doc, next_doc)):
            cols[n, at, :] = one_if(col_of[i] == doc).astype(BF16)


    def send_partials(g):
        half = pair.at[:, :, pl.ds(0, part), pl.ds(0, wide)]
        wait_bytes(half, own_sem.at[g])
        wait_bytes(half, pair_recv.at[g])
        tail, lead = cols[0, chip_rows, :], cols[1, chip_rows, :]
        for c in range(chips):
            for i in range(group):
                at = pl.ds((g * group + i) * DH, DH)
                part_out[g, c, i, 0] = tn(pair[K, c, :, at] * tail, pair[V, c, :, at]).astype(BF16)
                part_out[g, c, i, 1] = tn(pair[Q, c, :, at] * lead, pair[G, c, :, at]).astype(BF16)
        for step in range(1, chips):
            pltpu.make_async_remote_copy(
                src_ref=part_out.at[g, lax.rem(chip + step, chips)],
                dst_ref=part_in.at[g, chip],
                send_sem=part_send.at[g],
                recv_sem=part_recv.at[g],
                device_id=at_chip(step),
                device_id_type=MESH,
            ).start()
        part_in[g, chip] = part_out[g, chip]

    for g in range(groups):
        send_partials(g)

    def send_tokens(h, done=()):
        at = pl.ds(h * DH, DH)
        for a in range(4):
            for step in range(1, chips) if a not in done else ():
                pltpu.make_async_remote_copy(
                    src_ref=pair.at[a, lax.rem(chip + step, chips), :, at],
                    dst_ref=buf.at[a, chip_rows, at],
                    send_sem=tok_send.at[h],
                    recv_sem=tok_recv.at[h],
                    device_id=at_chip(step),
                    device_id_type=MESH,
                ).start()
            pltpu.make_async_copy(
                pair.at[a, chip, :, at], buf.at[a, chip_rows, at], mine_sem.at[h]
            ).start()

    send_tokens(0, EARLY)
    for h in range(1, heads):
        send_tokens(h)

    t_pos = lax.broadcasted_iota(jnp.int32, (128, 128), 0)
    s_pos = lax.broadcasted_iota(jnp.int32, (128, 128), 1)
    for i in range(per):
        at = slice(i * 128, (i + 1) * 128)
        for j in range(per):
            to = slice(j * 128, (j + 1) * 128)
            same = col_of[i] == row_of[j]
            allow[at, to] = one_if(same & (t_pos + i * 128 >= s_pos + j * 128)).astype(BF16)
            allow_t[at, to] = one_if(same & (t_pos + i * 128 <= s_pos + j * 128)).astype(BF16)

    base = me_z * ny
    before, after = last(jnp.maximum(base - 1, 0)), first(jnp.minimum(base + ny, blocks - 1))
    for y in range(ny):
        at = base + y
        keeps[0, y] = one_if(last(at) == last(jnp.maximum(at - 1, 0)))
        keeps[1, y] = one_if(first(at) == first(jnp.minimum(at + 1, blocks - 1)))
    for z in range(nz):
        keeps[2, z] = one_if((z < me_z) & (last(z * ny + ny - 1) == before))
        keeps[3, z] = one_if((z > me_z) & (first(z * ny) == after))

    def stage_states(g):
        wait_bytes(part_in.at[g, pl.ds(0, chips - 1)], part_recv.at[g])
        for i in range(group):
            for n in range(2):
                total = part_in[g, 0, i, n].astype(F32)
                for c in range(1, chips):
                    total = total + part_in[g, c, i, n].astype(F32)
                st[g, i, n] = total.astype(BF16)
        for step in range(1, ny):
            slot = pl.multiple_of(y_peer(step) * rows, rows)
            pltpu.make_async_remote_copy(
                src_ref=st.at[g, :, :, pl.ds(slot, rows), :],
                dst_ref=y_in.at[g, me_y],
                send_sem=y_send.at[g],
                recv_sem=y_recv.at[g],
                device_id=at_y(step),
                device_id_type=MESH,
            ).start()
        y_in[g, me_y] = st[g, :, :, pl.ds(pl.multiple_of(me_y * rows, rows), rows), :]

    def stage_totals(g):
        wait_bytes(y_in.at[g, pl.ds(0, ny - 1)], y_recv.at[g])
        total = y_in[g, 0, :, 0].astype(F32)
        for y in range(1, ny):
            total = y_in[g, y, :, 0].astype(F32) + keeps[0, y] * total
        z_out[g, 0] = total.astype(BF16)
        total = y_in[g, ny - 1, :, 1].astype(F32)
        for y in reversed(range(ny - 1)):
            total = y_in[g, y, :, 1].astype(F32) + keeps[1, y] * total
        z_out[g, 1] = total.astype(BF16)
        for step in range(1, nz):
            pltpu.make_async_remote_copy(
                src_ref=z_out.at[g, (me_z + step) // nz],
                dst_ref=z_in.at[g, me_z],
                send_sem=z_send.at[g],
                recv_sem=z_recv.at[g],
                device_id=at_z(step),
                device_id_type=MESH,
            ).start()
        z_in[g, me_z] = jnp.zeros((group, rows, DH), BF16)

    def stage_prefix(g):
        wait_bytes(z_in.at[g, pl.ds(0, nz - 1)], z_recv.at[g])
        state = jnp.zeros((group, rows, DH), F32)
        gstate = jnp.zeros((group, rows, DH), F32)
        for z in range(nz):
            term = z_in[g, z].astype(F32)
            state = state + keeps[2, z] * term
            gstate = gstate + keeps[3, z] * term
        for y in range(ny):
            p_out[g, y, :, 0] = state.astype(BF16)
            if y < ny - 1:
                state = y_in[g, y, :, 0].astype(F32) + keeps[0, y] * state
        for y in reversed(range(ny)):
            p_out[g, y, :, 1] = gstate.astype(BF16)
            if y > 0:
                gstate = y_in[g, y, :, 1].astype(F32) + keeps[1, y] * gstate
        here = pl.ds(pl.multiple_of(me_y * rows, rows), rows)
        for step in range(1, ny):
            pltpu.make_async_remote_copy(
                src_ref=p_out.at[g, y_peer(step)],
                dst_ref=held.at[g, :, :, here, :],
                send_sem=p_send.at[g],
                recv_sem=p_recv.at[g],
                device_id=at_y(step),
                device_id_type=MESH,
            ).start()
        held[g, :, :, here, :] = p_out[g, me_y]

    arrival, phase = 3.0 * group, 5.5
    stages = [(g * arrival + n * phase, n, g) for g in range(groups) for n in range(3)]

    @pl.when(core == 1)
    def _():
        pl.semaphore_wait(barrier, 2 * len(across))
        greet(cross_in, sibling)

    @pl.when(core == 0)
    def _():
        pl.semaphore_wait(cross_in, 1)

    for _, n, g in sorted(stages):
        (stage_states, stage_totals, stage_prefix)[n](g)

    tile = min(256, tok)

    def scores(h, left, right, by_row, by_col):
        here = pl.ds(pl.multiple_of(h * DH, DH), DH)
        for i in range(tok // tile):
            at, upto = slice(i * tile, (i + 1) * tile), slice(0, (i + 1) * tile)
            s = nt(buf[left, at, here], buf[right, upto, here]).astype(BF16) * allow[at, upto]
            acc[by_row[0], h, at, :] = nn(s, buf[by_row[1], upto, here])
            onward = slice(i * tile, tok)
            s = nt(buf[right, at, here], buf[left, onward, here]).astype(BF16) * allow_t[at, onward]
            acc[by_col[0], h, at, :] = nn(s, buf[by_col[1], onward, here])

    def intra(h, carry):
        wait_bytes(buf.at[:, pl.ds(0, both), pl.ds(0, DH)], mine_sem.at[h])
        wait_bytes(buf.at[:, pl.ds(0, tok - both), pl.ds(0, DH)], tok_recv.at[h])
        scores(h, Q, K, (0, V), (3, G))
        scores(h, G, V, (1, K), (2, Q))
        return carry

    def finish(h, carry):
        g, i = h // group, h % group
        here = pl.ds(pl.multiple_of(h * DH, DH), DH)
        state, gstate = held[g, i, 0], held[g, i, 1]
        match, back = cols[2], cols[3]
        out_ref[0, :, here] = (acc[0, h] + nn(buf[Q, :, here] * match, state)).astype(BF16)
        out_ref[1, :, here] = (acc[1, h] + nt(buf[G, :, here] * match, state)).astype(BF16)
        out_ref[2, :, here] = (acc[2, h] + nt(buf[V, :, here] * back, gstate)).astype(BF16)
        out_ref[3, :, here] = (acc[3, h] + nn(buf[K, :, here] * back, gstate)).astype(BF16)
        return carry

    ahead = heads - group
    lax.fori_loop(0, heads - 1, intra, 0)
    for g in range(groups - 1):
        wait_bytes(y_in.at[g, pl.ds(0, ny - 1)], p_recv.at[g])
    lax.fori_loop(0, ahead, finish, 0)
    lax.fori_loop(heads - 1, heads, intra, 0)
    wait_bytes(y_in.at[groups - 1, pl.ds(0, ny - 1)], p_recv.at[groups - 1])
    lax.fori_loop(ahead, heads, finish, 0)

    for g in range(groups):
        wait_bytes(pair.at[:, :, pl.ds(0, part), pl.ds(0, wide)], pair_send.at[g])
        wait_bytes(part_in.at[g, pl.ds(0, chips - 1)], part_send.at[g])
        wait_bytes(y_in.at[g, pl.ds(0, ny - 1)], y_send.at[g])
        wait_bytes(z_in.at[g, pl.ds(0, nz - 1)], z_send.at[g])
        wait_bytes(y_in.at[g, pl.ds(0, ny - 1)], p_send.at[g])
    for h in range(heads):
        wait_bytes(buf.at[:, pl.ds(0, tok - both), pl.ds(0, DH)], tok_send.at[h])


def shards(nx, ny, nz, queries, keys, values, out_grad, doc_ids):
    part, width = queries.shape
    tok = part * nx
    heads = width // DH // nx
    group = min(GROUP, heads)
    groups = heads // group
    chips = nx // 2
    rows = DH // ny
    docs = doc_ids.reshape(-1, 128)
    operands = [
        pltpu.with_memory_space_constraint(x, pltpu.HBM)
        for x in (queries, keys, values, out_grad, docs)
    ]
    dma = pltpu.SemaphoreType.DMA
    results = pl.pallas_call(
        functools.partial(kernel, nx, ny, nz, heads, tok, group),
        out_shape=pltpu.VMEM((4, tok, heads * DH), BF16),
        in_specs=[pl.BlockSpec(memory_space=pltpu.HBM)] * 5,
        out_specs=pl.BlockSpec(memory_space=pltpu.VMEM),
        scratch_shapes=[
            pltpu.VMEM((4, chips, 2 * part, heads * DH), BF16),
            pltpu.VMEM((4, tok, heads * DH), BF16),
            pltpu.VMEM((4, heads, tok, DH), F32),
            pltpu.VMEM((tok, tok), BF16),
            pltpu.VMEM((tok, tok), BF16),
            pltpu.VMEM((4, tok, DH), BF16),
            pltpu.VMEM(docs.shape, jnp.int32),
            pltpu.SMEM(docs.shape, jnp.int32),
            pltpu.SMEM((4, max(ny, nz)), F32),
            pltpu.VMEM((groups, chips, group, 2, DH, DH), BF16),
            pltpu.VMEM((groups, chips, group, 2, DH, DH), BF16),
            pltpu.VMEM((groups, group, 2, DH, DH), BF16),
            pltpu.VMEM((groups, ny, group, 2, rows, DH), BF16),
            pltpu.VMEM((groups, 2, group, rows, DH), BF16),
            pltpu.VMEM((groups, nz, group, rows, DH), BF16),
            pltpu.VMEM((groups, ny, group, 2, rows, DH), BF16),
            pltpu.VMEM((groups, group, 2, DH, DH), BF16),
            dma((2,)),
            dma((groups,)),
            dma((groups,)),
            dma((groups,)),
            dma((groups,)),
            dma((groups,)),
            pltpu.SemaphoreType.REGULAR,
            pltpu.SemaphoreType.REGULAR,
            dma((heads,)),
            dma((heads,)),
            dma((heads,)),
            dma((groups,)),
            dma((groups,)),
            dma((groups,)),
            dma((groups,)),
            dma((groups,)),
            dma((groups,)),
        ],
        compiler_params=pltpu.CompilerParams(
            collective_id=0, has_side_effects=True, vmem_limit_bytes=40 * 1024 * 1024
        ),
    )(*operands)
    return tuple(results[i] for i in range(4))


def solution(mesh):
    nx, blocks = mesh.shape["head"], mesh.shape["ctx"]
    ny = min(ROW, blocks)
    rows = P(("ctx", "head"), None)
    return jax.shard_map(
        functools.partial(shards, nx, ny, blocks // ny),
        mesh=mesh,
        in_specs=(rows, rows, rows, rows, P()),
        out_specs=(P("ctx", "head"),) * 4,
        check_vma=False,
    )
```

```python
import functools

import jax
import jax.numpy as jnp
from jax import lax
from jax.experimental import pallas as pl
from jax.experimental.pallas import tpu as pltpu
from jax.sharding import PartitionSpec as P

DH = 128
ROW = 8
GROUP = 1
FIRST = 0
MESH = pl.DeviceIdType.MESH
F32, BF16 = jnp.float32, jnp.bfloat16
K, V, Q, G = range(4)
EARLY = (K,)


def nt(a, b):
    return lax.dot_general(a, b, (((1,), (1,)), ((), ())), preferred_element_type=F32)


def nn(a, b):
    return lax.dot_general(a, b, (((1,), (0,)), ((), ())), preferred_element_type=F32)


def tn(a, b):
    return lax.dot_general(a, b, (((0,), (0,)), ((), ())), preferred_element_type=F32)


def one_if(flag):
    return jnp.where(flag, F32(1.0), F32(0.0))


def wait_bytes(ref, sem):
    if 0 not in ref.shape:
        pltpu.make_async_copy(ref, ref, sem).wait()


def kernel(
    nx, ny, nz, heads, tok, group,
    q_ref, k_ref, v_ref, g_ref, docs_ref,
    out_ref,
    pair, buf, acc, allow, allow_t, cols, docs_v, near_s, docs_s, keeps,
    part_out, part_in, relay_in, relay_out, st, y_in, z_out, z_in, p_out, held,
    docs_sem, own_sem, pair_send, pair_recv, part_send, part_recv, relay_send, relay_recv,
    line_in, cross_in, mine_sem, tok_send, tok_recv, y_send, y_recv, z_send, z_recv, p_send, p_recv,
):
    ctx = lax.axis_index("ctx")
    me_x = lax.axis_index("head")
    me_z, me_y = ctx // ny, ctx % ny
    chip, core = me_x // 2, me_x % 2
    chips = nx // 2
    groups = heads // group
    part = tok // nx
    both = 2 * part
    rows = DH // ny
    per = tok // 128
    blocks = ny * nz
    wide = group * DH

    def chip_at(step):
        return lax.rem(chip + step, chips)

    def at_chip(step):
        return {"head": chip_at(step) * 2 + core}

    def y_peer(step):
        return lax.rem(me_y + step, ny)

    def at_y(step):
        return {"ctx": me_z * ny + y_peer(step)}

    def at_z(step):
        return {"ctx": lax.rem(me_z + step, nz) * ny + me_y}

    sibling = {"head": me_x + 1 - 2 * core}
    sources = (k_ref, v_ref, q_ref, g_ref)
    own_rows = pl.ds(pl.multiple_of(core * part, part), part)

    def columns(owner, first):
        return pl.ds(pl.multiple_of((owner * heads + first) * DH, DH), wide)

    row_docs = pl.ds(pl.multiple_of(me_z * ny * per, ny * per), ny * per)
    docs_copies = [
        pltpu.make_async_copy(docs_ref.at[row_docs], near_s, docs_sem.at[0]),
        pltpu.make_async_copy(docs_ref.at[row_docs], docs_v, docs_sem.at[1]),
        pltpu.make_async_copy(docs_ref, docs_s, docs_sem.at[2]),
    ]
    for copy in docs_copies:
        copy.start()
    for g in range(groups):
        for a in range(4):
            for c in range(chips):
                pltpu.make_async_copy(
                    sources[a].at[:, columns(c * 2 + core, g * group)],
                    pair.at[a, c, own_rows, pl.ds(g * wide, wide)],
                    own_sem.at[g],
                ).start()

    barrier = pltpu.get_barrier_semaphore()

    def greet(sem, peer):
        pl.semaphore_signal(sem, inc=1, device_id=peer, device_id_type=MESH)

    for step in range(1, chips):
        greet(barrier, {"head": lax.rem(chip + step, chips) * 2 + 1})
    pl.when(core == 0)(lambda: greet(barrier, sibling))
    across = [at_y(step) for step in range(1, ny)] + [at_z(step) for step in range(1, nz)]
    for peer in across:
        greet(barrier, {**peer, "head": chip * 2})

    @pl.when(core == 1)
    def _():
        pl.semaphore_wait(barrier, nx - 1)
        greet(line_in, sibling)

    @pl.when(core == 0)
    def _():
        pl.semaphore_wait(line_in, 1)

    for g in range(groups):
        for a in range(4):
            for c in range(chips):
                pltpu.make_async_remote_copy(
                    src_ref=sources[a].at[:, columns(c * 2 + 1 - core, g * group)],
                    dst_ref=pair.at[a, c, own_rows, pl.ds(g * wide, wide)],
                    send_sem=pair_send.at[g],
                    recv_sem=pair_recv.at[g],
                    device_id=sibling,
                    device_id_type=MESH,
                ).start()

    chip_rows = pl.ds(pl.multiple_of(chip * both, both), both)
    mine = pl.ds(pl.multiple_of(me_x * part, part), part)
    for a in EARLY:
        for step in range(1, chips):
            there = lax.rem(chip + step, chips) * 2
            for c in range(2):
                pltpu.make_async_remote_copy(
                    src_ref=sources[a].at[:, pl.ds(pl.multiple_of((there + c) * heads * DH, DH), DH)],
                    dst_ref=buf.at[a, mine, pl.ds(0, DH)],
                    send_sem=tok_send.at[0],
                    recv_sem=tok_recv.at[0],
                    device_id={"head": there + c},
                    device_id_type=MESH,
                ).start()

    for copy in docs_copies[:2]:
        copy.wait()

    def mark(n, doc):
        for i in range(per):
            cols[n, i * 128 : (i + 1) * 128, :] = one_if(col_of[i] == doc).astype(BF16)

    local = docs_v[pl.ds(pl.multiple_of(me_y * per, per), per), :]
    row_of = [jnp.broadcast_to(local[i : i + 1, :], (128, 128)) for i in range(per)]
    col_of = [r.T for r in row_of]
    mark(0, near_s[me_y * per + per - 1, 127])
    mark(1, near_s[me_y * per, 0])


    def send_partials(g):
        half = pair.at[:, :, pl.ds(0, part), pl.ds(0, wide)]
        wait_bytes(half, own_sem.at[g])
        wait_bytes(half, pair_recv.at[g])
        tail, lead = cols[0, chip_rows, :], cols[1, chip_rows, :]
        for c in range(chips):
            for i in range(group):
                at = pl.ds((g * group + i) * DH, DH)
                part_out[g, c, i, 0] = tn(pair[K, c, :, at] * tail, pair[V, c, :, at]).astype(BF16)
                part_out[g, c, i, 1] = tn(pair[Q, c, :, at] * lead, pair[G, c, :, at]).astype(BF16)
        for n in range(2):
            near, far = (1, chips - 1) if n == 0 else (chips - 1, 1)
            pltpu.make_async_remote_copy(
                src_ref=part_out.at[g, chip_at(2), :, n],
                dst_ref=relay_in.at[g, n],
                send_sem=part_send.at[g],
                recv_sem=relay_recv.at[g],
                device_id=at_chip(near),
                device_id_type=MESH,
            ).start()
            pltpu.make_async_remote_copy(
                src_ref=part_out.at[g, chip_at(far), :, n],
                dst_ref=part_in.at[g, 0, :, n],
                send_sem=part_send.at[g],
                recv_sem=part_recv.at[g],
                device_id=at_chip(far),
                device_id_type=MESH,
            ).start()

    def relay_partials(g):
        wait_bytes(relay_in.at[g], relay_recv.at[g])
        for n in range(2):
            near = 1 if n == 0 else chips - 1
            relay_out[g, n] = (
                part_out[g, chip_at(near), :, n].astype(F32) + relay_in[g, n].astype(F32)
            ).astype(BF16)
            pltpu.make_async_remote_copy(
                src_ref=relay_out.at[g, n],
                dst_ref=part_in.at[g, 1, :, n],
                send_sem=relay_send.at[g],
                recv_sem=part_recv.at[g],
                device_id=at_chip(near),
                device_id_type=MESH,
            ).start()

    def send_tokens(h, arrays=range(4)):
        at = pl.ds(h * DH, DH)
        for a in arrays:
            for step in range(1, chips):
                pltpu.make_async_remote_copy(
                    src_ref=pair.at[a, chip_at(step), :, at],
                    dst_ref=buf.at[a, chip_rows, at],
                    send_sem=tok_send.at[h],
                    recv_sem=tok_recv.at[h],
                    device_id=at_chip(step),
                    device_id_type=MESH,
                ).start()

    for g in range(groups):
        send_partials(g)
    rest = [a for a in range(4) if a not in EARLY]
    send_tokens(0, rest[:FIRST])
    for g in range(groups):
        relay_partials(g)
    send_tokens(0, rest[FIRST:])
    for h in range(1, heads):
        send_tokens(h)
    for h in range(heads):
        at = pl.ds(h * DH, DH)
        for a in range(4):
            pltpu.make_async_copy(
                pair.at[a, chip, :, at], buf.at[a, chip_rows, at], mine_sem.at[h]
            ).start()

    t_pos = lax.broadcasted_iota(jnp.int32, (128, 128), 0)
    s_pos = lax.broadcasted_iota(jnp.int32, (128, 128), 1)
    for i in range(per):
        at = slice(i * 128, (i + 1) * 128)
        for j in range(per):
            to = slice(j * 128, (j + 1) * 128)
            same = col_of[i] == row_of[j]
            allow[at, to] = one_if(same & (t_pos + i * 128 >= s_pos + j * 128)).astype(BF16)
            allow_t[at, to] = one_if(same & (t_pos + i * 128 <= s_pos + j * 128)).astype(BF16)

    docs_copies[2].wait()

    def last(block):
        return docs_s[block * per + per - 1, 127]

    def first(block):
        return docs_s[block * per, 0]

    mark(2, jnp.where(ctx == 0, -1, last(jnp.maximum(ctx - 1, 0))))
    mark(3, jnp.where(ctx == blocks - 1, -1, first(jnp.minimum(ctx + 1, blocks - 1))))

    base = me_z * ny
    before, after = last(jnp.maximum(base - 1, 0)), first(jnp.minimum(base + ny, blocks - 1))
    for y in range(ny):
        at = base + y
        keeps[0, y] = one_if(last(at) == last(jnp.maximum(at - 1, 0)))
        keeps[1, y] = one_if(first(at) == first(jnp.minimum(at + 1, blocks - 1)))
    for z in range(nz):
        keeps[2, z] = one_if((z < me_z) & (last(z * ny + ny - 1) == before))
        keeps[3, z] = one_if((z > me_z) & (first(z * ny) == after))

    def stage_states(g):
        wait_bytes(part_in.at[g], part_recv.at[g])
        for i in range(group):
            for n in range(2):
                total = part_out[g, chip, i, n].astype(F32)
                for c in range(2):
                    total = total + part_in[g, c, i, n].astype(F32)
                st[g, i, n] = total.astype(BF16)
        for step in range(1, ny):
            slot = pl.multiple_of(y_peer(step) * rows, rows)
            pltpu.make_async_remote_copy(
                src_ref=st.at[g, :, :, pl.ds(slot, rows), :],
                dst_ref=y_in.at[g, me_y],
                send_sem=y_send.at[g],
                recv_sem=y_recv.at[g],
                device_id=at_y(step),
                device_id_type=MESH,
            ).start()
        y_in[g, me_y] = st[g, :, :, pl.ds(pl.multiple_of(me_y * rows, rows), rows), :]

    def stage_totals(g):
        wait_bytes(y_in.at[g, pl.ds(0, ny - 1)], y_recv.at[g])
        total = y_in[g, 0, :, 0].astype(F32)
        for y in range(1, ny):
            total = y_in[g, y, :, 0].astype(F32) + keeps[0, y] * total
        z_out[g, 0] = total.astype(BF16)
        total = y_in[g, ny - 1, :, 1].astype(F32)
        for y in reversed(range(ny - 1)):
            total = y_in[g, y, :, 1].astype(F32) + keeps[1, y] * total
        z_out[g, 1] = total.astype(BF16)
        for step in range(1, nz):
            pltpu.make_async_remote_copy(
                src_ref=z_out.at[g, (me_z + step) // nz],
                dst_ref=z_in.at[g, me_z],
                send_sem=z_send.at[g],
                recv_sem=z_recv.at[g],
                device_id=at_z(step),
                device_id_type=MESH,
            ).start()
        z_in[g, me_z] = jnp.zeros((group, rows, DH), BF16)

    def stage_prefix(g):
        wait_bytes(z_in.at[g, pl.ds(0, nz - 1)], z_recv.at[g])
        state = jnp.zeros((group, rows, DH), F32)
        gstate = jnp.zeros((group, rows, DH), F32)
        for z in range(nz):
            term = z_in[g, z].astype(F32)
            state = state + keeps[2, z] * term
            gstate = gstate + keeps[3, z] * term
        for y in range(ny):
            p_out[g, y, :, 0] = state.astype(BF16)
            if y < ny - 1:
                state = y_in[g, y, :, 0].astype(F32) + keeps[0, y] * state
        for y in reversed(range(ny)):
            p_out[g, y, :, 1] = gstate.astype(BF16)
            if y > 0:
                gstate = y_in[g, y, :, 1].astype(F32) + keeps[1, y] * gstate
        here = pl.ds(pl.multiple_of(me_y * rows, rows), rows)
        for step in range(1, ny):
            pltpu.make_async_remote_copy(
                src_ref=p_out.at[g, y_peer(step)],
                dst_ref=held.at[g, :, :, here, :],
                send_sem=p_send.at[g],
                recv_sem=p_recv.at[g],
                device_id=at_y(step),
                device_id_type=MESH,
            ).start()
        held[g, :, :, here, :] = p_out[g, me_y]

    arrival, phase = 1.3 * group, 5.5
    stages = [(g * arrival + n * phase, n, g) for g in range(groups) for n in range(3)]

    @pl.when(core == 0)
    def _():
        pl.semaphore_wait(barrier, 2 * len(across))
        greet(cross_in, sibling)

    @pl.when(core == 1)
    def _():
        pl.semaphore_wait(cross_in, 1)

    for _, n, g in sorted(stages):
        (stage_states, stage_totals, stage_prefix)[n](g)

    tile = min(256, tok)

    def scores(h, left, right, by_row, by_col):
        here = pl.ds(pl.multiple_of(h * DH, DH), DH)
        for i in range(tok // tile):
            at, upto = slice(i * tile, (i + 1) * tile), slice(0, (i + 1) * tile)
            s = nt(buf[left, at, here], buf[right, upto, here]).astype(BF16) * allow[at, upto]
            acc[by_row[0], h, at, :] = nn(s, buf[by_row[1], upto, here])
            onward = slice(i * tile, tok)
            s = nt(buf[right, at, here], buf[left, onward, here]).astype(BF16) * allow_t[at, onward]
            acc[by_col[0], h, at, :] = nn(s, buf[by_col[1], onward, here])

    def intra(h, carry):
        wait_bytes(buf.at[:, pl.ds(0, both), pl.ds(0, DH)], mine_sem.at[h])
        wait_bytes(buf.at[:, pl.ds(0, tok - both), pl.ds(0, DH)], tok_recv.at[h])
        scores(h, Q, K, (0, V), (3, G))
        scores(h, G, V, (1, K), (2, Q))
        return carry

    def finish(h, carry):
        g, i = h // group, h % group
        here = pl.ds(pl.multiple_of(h * DH, DH), DH)
        state, gstate = held[g, i, 0], held[g, i, 1]
        match, back = cols[2], cols[3]
        out_ref[0, :, here] = (acc[0, h] + nn(buf[Q, :, here] * match, state)).astype(BF16)
        out_ref[1, :, here] = (acc[1, h] + nt(buf[G, :, here] * match, state)).astype(BF16)
        out_ref[2, :, here] = (acc[2, h] + nt(buf[V, :, here] * back, gstate)).astype(BF16)
        out_ref[3, :, here] = (acc[3, h] + nn(buf[K, :, here] * back, gstate)).astype(BF16)
        return carry

    ahead = heads - group
    lax.fori_loop(0, heads - 1, intra, 0)
    for g in range(groups - 1):
        wait_bytes(y_in.at[g, pl.ds(0, ny - 1)], p_recv.at[g])
    lax.fori_loop(0, ahead, finish, 0)
    lax.fori_loop(heads - 1, heads, intra, 0)
    wait_bytes(y_in.at[groups - 1, pl.ds(0, ny - 1)], p_recv.at[groups - 1])
    lax.fori_loop(ahead, heads, finish, 0)

    for g in range(groups):
        wait_bytes(pair.at[:, :, pl.ds(0, part), pl.ds(0, wide)], pair_send.at[g])
        wait_bytes(part_in.at[g], part_send.at[g])
        wait_bytes(relay_in.at[g], relay_send.at[g])
        wait_bytes(y_in.at[g, pl.ds(0, ny - 1)], y_send.at[g])
        wait_bytes(z_in.at[g, pl.ds(0, nz - 1)], z_send.at[g])
        wait_bytes(y_in.at[g, pl.ds(0, ny - 1)], p_send.at[g])
    for h in range(heads):
        wait_bytes(buf.at[:, pl.ds(0, tok - both), pl.ds(0, DH)], tok_send.at[h])


def shards(nx, ny, nz, queries, keys, values, out_grad, doc_ids):
    part, width = queries.shape
    tok = part * nx
    heads = width // DH // nx
    group = min(GROUP, heads)
    groups = heads // group
    chips = nx // 2
    rows = DH // ny
    docs = doc_ids.reshape(-1, 128)
    operands = [
        pltpu.with_memory_space_constraint(x, pltpu.HBM)
        for x in (queries, keys, values, out_grad, docs)
    ]
    dma = pltpu.SemaphoreType.DMA
    results = pl.pallas_call(
        functools.partial(kernel, nx, ny, nz, heads, tok, group),
        out_shape=pltpu.VMEM((4, tok, heads * DH), BF16),
        in_specs=[pl.BlockSpec(memory_space=pltpu.HBM)] * 5,
        out_specs=pl.BlockSpec(memory_space=pltpu.VMEM),
        scratch_shapes=[
            pltpu.VMEM((4, chips, 2 * part, heads * DH), BF16),
            pltpu.VMEM((4, tok, heads * DH), BF16),
            pltpu.VMEM((4, heads, tok, DH), F32),
            pltpu.VMEM((tok, tok), BF16),
            pltpu.VMEM((tok, tok), BF16),
            pltpu.VMEM((4, tok, DH), BF16),
            pltpu.VMEM((ny * tok // 128, 128), jnp.int32),
            pltpu.SMEM((ny * tok // 128, 128), jnp.int32),
            pltpu.SMEM(docs.shape, jnp.int32),
            pltpu.SMEM((4, max(ny, nz)), F32),
            pltpu.VMEM((groups, chips, group, 2, DH, DH), BF16),
            pltpu.VMEM((groups, 2, group, 2, DH, DH), BF16),
            pltpu.VMEM((groups, 2, group, DH, DH), BF16),
            pltpu.VMEM((groups, 2, group, DH, DH), BF16),
            pltpu.VMEM((groups, group, 2, DH, DH), BF16),
            pltpu.VMEM((groups, ny, group, 2, rows, DH), BF16),
            pltpu.VMEM((groups, 2, group, rows, DH), BF16),
            pltpu.VMEM((groups, nz, group, rows, DH), BF16),
            pltpu.VMEM((groups, ny, group, 2, rows, DH), BF16),
            pltpu.VMEM((groups, group, 2, DH, DH), BF16),
            dma((3,)),
            dma((groups,)),
            dma((groups,)),
            dma((groups,)),
            dma((groups,)),
            dma((groups,)),
            dma((groups,)),
            dma((groups,)),
            pltpu.SemaphoreType.REGULAR,
            pltpu.SemaphoreType.REGULAR,
            dma((heads,)),
            dma((heads,)),
            dma((heads,)),
            dma((groups,)),
            dma((groups,)),
            dma((groups,)),
            dma((groups,)),
            dma((groups,)),
            dma((groups,)),
        ],
        compiler_params=pltpu.CompilerParams(
            collective_id=0, has_side_effects=True, vmem_limit_bytes=40 * 1024 * 1024
        ),
    )(*operands)
    return tuple(results[i] for i in range(4))


def solution(mesh):
    nx, blocks = mesh.shape["head"], mesh.shape["ctx"]
    ny = min(ROW, blocks)
    rows = P(("ctx", "head"), None)
    return jax.shard_map(
        functools.partial(shards, nx, ny, blocks // ny),
        mesh=mesh,
        in_specs=(rows, rows, rows, rows, P()),
        out_specs=(P("ctx", "head"),) * 4,
        check_vma=False,
    )
```

```python
import functools

import jax
import jax.numpy as jnp
from jax import lax
from jax.experimental import pallas as pl
from jax.experimental.pallas import tpu as pltpu
from jax.sharding import PartitionSpec as P

DH = 128
ROW = 8
GROUP = 1
FIRST = 0
MESH = pl.DeviceIdType.MESH
F32, BF16 = jnp.float32, jnp.bfloat16
K, V, Q, G = range(4)
EARLY = (K,)


def nt(a, b):
    return lax.dot_general(a, b, (((1,), (1,)), ((), ())), preferred_element_type=F32)


def nn(a, b):
    return lax.dot_general(a, b, (((1,), (0,)), ((), ())), preferred_element_type=F32)


def tn(a, b):
    return lax.dot_general(a, b, (((0,), (0,)), ((), ())), preferred_element_type=F32)


def one_if(flag):
    return jnp.where(flag, F32(1.0), F32(0.0))


def far_first(count):
    return sorted(range(1, count), key=lambda step: -min(step, count - step))


def wait_bytes(ref, sem):
    if 0 not in ref.shape:
        pltpu.make_async_copy(ref, ref, sem).wait()


def kernel(
    nx, ny, nz, heads, tok, group,
    q_ref, k_ref, v_ref, g_ref, docs_ref,
    out_ref,
    pair, buf, acc, allow, allow_t, cols, docs_v, near_s, docs_s, keeps,
    part_out, part_in, relay_in, relay_out, st, y_in, z_out, z_in, p_out, held,
    docs_sem, own_sem, pair_send, pair_recv, part_send, part_recv, relay_send, relay_recv,
    line_in, cross_in, mine_sem, tok_send, tok_recv, y_send, y_recv, z_send, z_recv, p_send, p_recv,
):
    ctx = lax.axis_index("ctx")
    me_x = lax.axis_index("head")
    me_z, me_y = ctx // ny, ctx % ny
    chip, core = me_x // 2, me_x % 2
    chips = nx // 2
    groups = heads // group
    early = list(range(1, groups))
    turns = early + [0]
    part = tok // nx
    both = 2 * part
    rows = DH // ny
    per = tok // 128
    blocks = ny * nz
    wide = group * DH

    def chip_at(step):
        return lax.rem(chip + step, chips)

    def at_chip(step):
        return {"head": chip_at(step) * 2 + core}

    def y_peer(step):
        return lax.rem(me_y + step, ny)

    def at_y(step):
        return {"ctx": me_z * ny + y_peer(step)}

    def at_z(step):
        return {"ctx": lax.rem(me_z + step, nz) * ny + me_y}

    sibling = {"head": me_x + 1 - 2 * core}
    sources = (k_ref, v_ref, q_ref, g_ref)
    own_rows = pl.ds(pl.multiple_of(core * part, part), part)

    def columns(owner, first):
        return pl.ds(pl.multiple_of((owner * heads + first) * DH, DH), wide)

    row_docs = pl.ds(pl.multiple_of(me_z * ny * per, ny * per), ny * per)
    docs_copies = [
        pltpu.make_async_copy(docs_ref.at[row_docs], near_s, docs_sem.at[0]),
        pltpu.make_async_copy(docs_ref.at[row_docs], docs_v, docs_sem.at[1]),
        pltpu.make_async_copy(docs_ref, docs_s, docs_sem.at[2]),
    ]
    for copy in docs_copies:
        copy.start()
    for g in turns:
        for a in range(4):
            for c in range(chips):
                pltpu.make_async_copy(
                    sources[a].at[:, columns(c * 2 + core, g * group)],
                    pair.at[a, c, own_rows, pl.ds(g * wide, wide)],
                    own_sem.at[g],
                ).start()

    barrier = pltpu.get_barrier_semaphore()

    def greet(sem, peer):
        pl.semaphore_signal(sem, inc=1, device_id=peer, device_id_type=MESH)

    for step in range(1, chips):
        greet(barrier, {"head": lax.rem(chip + step, chips) * 2 + 1})
    pl.when(core == 0)(lambda: greet(barrier, sibling))
    across = [at_y(step) for step in range(1, ny)] + [at_z(step) for step in range(1, nz)]
    for peer in across:
        greet(barrier, {**peer, "head": chip * 2})

    @pl.when(core == 1)
    def _():
        pl.semaphore_wait(barrier, nx - 1)
        greet(line_in, sibling)

    @pl.when(core == 0)
    def _():
        pl.semaphore_wait(line_in, 1)

    for g in turns:
        for a in range(4):
            for c in range(chips):
                pltpu.make_async_remote_copy(
                    src_ref=sources[a].at[:, columns(c * 2 + 1 - core, g * group)],
                    dst_ref=pair.at[a, c, own_rows, pl.ds(g * wide, wide)],
                    send_sem=pair_send.at[g],
                    recv_sem=pair_recv.at[g],
                    device_id=sibling,
                    device_id_type=MESH,
                ).start()

    chip_rows = pl.ds(pl.multiple_of(chip * both, both), both)
    mine = pl.ds(pl.multiple_of(me_x * part, part), part)
    for a in EARLY:
        for step in range(1, chips):
            there = lax.rem(chip + step, chips) * 2
            for c in range(2):
                pltpu.make_async_remote_copy(
                    src_ref=sources[a].at[:, pl.ds(pl.multiple_of((there + c) * heads * DH, DH), DH)],
                    dst_ref=buf.at[a, mine, pl.ds(0, DH)],
                    send_sem=tok_send.at[0],
                    recv_sem=tok_recv.at[heads if a in (K, V) else 0],
                    device_id={"head": there + c},
                    device_id_type=MESH,
                ).start()

    for copy in docs_copies[:2]:
        copy.wait()

    def mark(n, doc):
        for i in range(per):
            cols[n, i * 128 : (i + 1) * 128, :] = one_if(col_of[i] == doc).astype(BF16)

    local = docs_v[pl.ds(pl.multiple_of(me_y * per, per), per), :]
    row_of = [jnp.broadcast_to(local[i : i + 1, :], (128, 128)) for i in range(per)]
    col_of = [r.T for r in row_of]
    mark(0, near_s[me_y * per + per - 1, 127])
    mark(1, near_s[me_y * per, 0])


    def wait_pair(g):
        half = pair.at[:, :, pl.ds(0, part), pl.ds(0, wide)]
        wait_bytes(half, own_sem.at[g])
        wait_bytes(half, pair_recv.at[g])

    def send_partials(g):
        wait_pair(g)
        tail, lead = cols[0, chip_rows, :], cols[1, chip_rows, :]
        for c in range(chips):
            for i in range(group):
                at = pl.ds((g * group + i) * DH, DH)
                part_out[g, c, i, 0] = tn(pair[K, c, :, at] * tail, pair[V, c, :, at]).astype(BF16)
                part_out[g, c, i, 1] = tn(pair[Q, c, :, at] * lead, pair[G, c, :, at]).astype(BF16)
        for n in range(2):
            near, far = (1, chips - 1) if n == 0 else (chips - 1, 1)
            pltpu.make_async_remote_copy(
                src_ref=part_out.at[g, chip_at(2), :, n],
                dst_ref=relay_in.at[g, n],
                send_sem=part_send.at[g],
                recv_sem=relay_recv.at[g],
                device_id=at_chip(near),
                device_id_type=MESH,
            ).start()
            pltpu.make_async_remote_copy(
                src_ref=part_out.at[g, chip_at(far), :, n],
                dst_ref=part_in.at[g, 0, :, n],
                send_sem=part_send.at[g],
                recv_sem=part_recv.at[g],
                device_id=at_chip(far),
                device_id_type=MESH,
            ).start()

    def relay_partials(g):
        wait_bytes(relay_in.at[g], relay_recv.at[g])
        for n in range(2):
            near = 1 if n == 0 else chips - 1
            relay_out[g, n] = (
                part_out[g, chip_at(near), :, n].astype(F32) + relay_in[g, n].astype(F32)
            ).astype(BF16)
            pltpu.make_async_remote_copy(
                src_ref=relay_out.at[g, n],
                dst_ref=part_in.at[g, 1, :, n],
                send_sem=relay_send.at[g],
                recv_sem=part_recv.at[g],
                device_id=at_chip(near),
                device_id_type=MESH,
            ).start()

    def send_tokens(h, arrays=range(4)):
        at = pl.ds(h * DH, DH)
        for a in arrays:
            for step in range(1, chips):
                pltpu.make_async_remote_copy(
                    src_ref=pair.at[a, chip_at(step), :, at],
                    dst_ref=buf.at[a, chip_rows, at],
                    send_sem=tok_send.at[h],
                    recv_sem=tok_recv.at[heads if h == 0 and a in (K, V) else h],
                    device_id=at_chip(step),
                    device_id_type=MESH,
                ).start()

    for g in early:
        send_partials(g)
    wait_pair(0)
    rest = [a for a in range(4) if a not in EARLY]
    send_tokens(0, rest[:FIRST])
    for g in early:
        relay_partials(g)
    send_tokens(0, rest[FIRST:])
    for h in range(1, heads):
        send_tokens(h)
    for h in range(heads):
        at = pl.ds(h * DH, DH)
        for a in range(4):
            pltpu.make_async_copy(
                pair.at[a, chip, :, at], buf.at[a, chip_rows, at], mine_sem.at[h]
            ).start()

    t_pos = lax.broadcasted_iota(jnp.int32, (128, 128), 0)
    s_pos = lax.broadcasted_iota(jnp.int32, (128, 128), 1)
    for i in range(per):
        at = slice(i * 128, (i + 1) * 128)
        for j in range(per):
            to = slice(j * 128, (j + 1) * 128)
            same = col_of[i] == row_of[j]
            allow[at, to] = one_if(same & (t_pos + i * 128 >= s_pos + j * 128)).astype(BF16)
            allow_t[at, to] = one_if(same & (t_pos + i * 128 <= s_pos + j * 128)).astype(BF16)

    docs_copies[2].wait()

    def last(block):
        return docs_s[block * per + per - 1, 127]

    def first(block):
        return docs_s[block * per, 0]

    mark(2, jnp.where(ctx == 0, -1, last(jnp.maximum(ctx - 1, 0))))
    mark(3, jnp.where(ctx == blocks - 1, -1, first(jnp.minimum(ctx + 1, blocks - 1))))

    base = me_z * ny
    before, after = last(jnp.maximum(base - 1, 0)), first(jnp.minimum(base + ny, blocks - 1))
    for y in range(ny):
        at = base + y
        keeps[0, y] = one_if(last(at) == last(jnp.maximum(at - 1, 0)))
        keeps[1, y] = one_if(first(at) == first(jnp.minimum(at + 1, blocks - 1)))
    for z in range(nz):
        keeps[2, z] = one_if((z < me_z) & (last(z * ny + ny - 1) == before))
        keeps[3, z] = one_if((z > me_z) & (first(z * ny) == after))

    def wait_tokens(h):
        wait_bytes(buf.at[:, pl.ds(0, both), pl.ds(0, DH)], mine_sem.at[h])
        wait_bytes(buf.at[:, pl.ds(0, tok - both), pl.ds(0, DH)], tok_recv.at[h])

    def stage_states(g):
        if g in early:
            wait_bytes(part_in.at[g], part_recv.at[g])
            for i in range(group):
                for n in range(2):
                    total = part_out[g, chip, i, n].astype(F32)
                    for c in range(2):
                        total = total + part_in[g, c, i, n].astype(F32)
                    st[g, i, n] = total.astype(BF16)
        else:
            for i in range(group):
                at = pl.ds((g * group + i) * DH, DH)
                wait_bytes(buf.at[:, pl.ds(0, both), pl.ds(0, DH)], mine_sem.at[0])
                wait_bytes(buf.at[pl.ds(0, 2), pl.ds(0, tok - both), pl.ds(0, DH)], tok_recv.at[heads])
                st[g, i, 0] = tn(buf[K, :, at] * cols[0], buf[V, :, at]).astype(BF16)
                wait_bytes(buf.at[pl.ds(0, 2), pl.ds(0, tok - both), pl.ds(0, DH)], tok_recv.at[0])
                st[g, i, 1] = tn(buf[Q, :, at] * cols[1], buf[G, :, at]).astype(BF16)
        for step in far_first(ny):
            slot = pl.multiple_of(y_peer(step) * rows, rows)
            pltpu.make_async_remote_copy(
                src_ref=st.at[g, :, :, pl.ds(slot, rows), :],
                dst_ref=y_in.at[g, me_y],
                send_sem=y_send.at[g],
                recv_sem=y_recv.at[g],
                device_id=at_y(step),
                device_id_type=MESH,
            ).start()
        y_in[g, me_y] = st[g, :, :, pl.ds(pl.multiple_of(me_y * rows, rows), rows), :]

    def stage_totals(g):
        wait_bytes(y_in.at[g, pl.ds(0, ny - 1)], y_recv.at[g])
        total = y_in[g, 0, :, 0].astype(F32)
        for y in range(1, ny):
            total = y_in[g, y, :, 0].astype(F32) + keeps[0, y] * total
        z_out[g, 0] = total.astype(BF16)
        total = y_in[g, ny - 1, :, 1].astype(F32)
        for y in reversed(range(ny - 1)):
            total = y_in[g, y, :, 1].astype(F32) + keeps[1, y] * total
        z_out[g, 1] = total.astype(BF16)
        for step in far_first(nz):
            pltpu.make_async_remote_copy(
                src_ref=z_out.at[g, (me_z + step) // nz],
                dst_ref=z_in.at[g, me_z],
                send_sem=z_send.at[g],
                recv_sem=z_recv.at[g],
                device_id=at_z(step),
                device_id_type=MESH,
            ).start()
        z_in[g, me_z] = jnp.zeros((group, rows, DH), BF16)

    def stage_prefix(g):
        wait_bytes(z_in.at[g, pl.ds(0, nz - 1)], z_recv.at[g])
        state = jnp.zeros((group, rows, DH), F32)
        gstate = jnp.zeros((group, rows, DH), F32)
        for z in range(nz):
            term = z_in[g, z].astype(F32)
            state = state + keeps[2, z] * term
            gstate = gstate + keeps[3, z] * term
        for y in range(ny):
            p_out[g, y, :, 0] = state.astype(BF16)
            if y < ny - 1:
                state = y_in[g, y, :, 0].astype(F32) + keeps[0, y] * state
        for y in reversed(range(ny)):
            p_out[g, y, :, 1] = gstate.astype(BF16)
            if y > 0:
                gstate = y_in[g, y, :, 1].astype(F32) + keeps[1, y] * gstate
        here = pl.ds(pl.multiple_of(me_y * rows, rows), rows)
        for step in far_first(ny):
            pltpu.make_async_remote_copy(
                src_ref=p_out.at[g, y_peer(step)],
                dst_ref=held.at[g, :, :, here, :],
                send_sem=p_send.at[g],
                recv_sem=p_recv.at[g],
                device_id=at_y(step),
                device_id_type=MESH,
            ).start()
        held[g, :, :, here, :] = p_out[g, me_y]

    tile = min(256, tok)

    def scores(h, left, right, by_row, by_col):
        here = pl.ds(pl.multiple_of(h * DH, DH), DH)
        for i in range(tok // tile):
            at, upto = slice(i * tile, (i + 1) * tile), slice(0, (i + 1) * tile)
            s = nt(buf[left, at, here], buf[right, upto, here]).astype(BF16) * allow[at, upto]
            acc[by_row[0], h, at, :] = nn(s, buf[by_row[1], upto, here])
            onward = slice(i * tile, tok)
            s = nt(buf[right, at, here], buf[left, onward, here]).astype(BF16) * allow_t[at, onward]
            acc[by_col[0], h, at, :] = nn(s, buf[by_col[1], onward, here])

    def intra(h, carry):
        pl.when(h >= group)(lambda: wait_tokens(h))
        scores(h, Q, K, (0, V), (3, G))
        scores(h, G, V, (1, K), (2, Q))
        return carry

    def finish(h):
        g, i = h // group, h % group
        if i == 0:
            wait_bytes(y_in.at[g, pl.ds(0, ny - 1)], p_recv.at[g])
        here = pl.ds(h * DH, DH)
        state, gstate = held[g, i, 0], held[g, i, 1]
        match, back = cols[2], cols[3]
        out_ref[0, :, here] = (acc[0, h] + nn(buf[Q, :, here] * match, state)).astype(BF16)
        out_ref[1, :, here] = (acc[1, h] + nt(buf[G, :, here] * match, state)).astype(BF16)
        out_ref[2, :, here] = (acc[2, h] + nt(buf[V, :, here] * back, gstate)).astype(BF16)
        out_ref[3, :, here] = (acc[3, h] + nn(buf[K, :, here] * back, gstate)).astype(BF16)

    @pl.when(core == 0)
    def _():
        pl.semaphore_wait(barrier, 2 * len(across))
        greet(cross_in, sibling)

    @pl.when(core == 1)
    def _():
        pl.semaphore_wait(cross_in, 1)

    for g in early:
        stage_states(g)
    stage_totals(early[0])
    stage_states(0)
    for g in early[1:] + [0]:
        stage_totals(g)
    lax.fori_loop(0, 2, intra, 0)
    for g in turns:
        stage_prefix(g)
    lax.fori_loop(2, 3, intra, 0)
    for h in (1, 2):
        finish(h)
    lax.fori_loop(3, 4, intra, 0)
    for g in range(groups):
        wait_bytes(pair.at[:, :, pl.ds(0, part), pl.ds(0, wide)], pair_send.at[g])
        if g in early:
            wait_bytes(part_in.at[g], part_send.at[g])
            wait_bytes(relay_in.at[g], relay_send.at[g])
        wait_bytes(y_in.at[g, pl.ds(0, ny - 1)], y_send.at[g])
        wait_bytes(z_in.at[g, pl.ds(0, nz - 1)], z_send.at[g])
    for h in range(heads):
        wait_bytes(buf.at[:, pl.ds(0, tok - both), pl.ds(0, DH)], tok_send.at[h])
    for h in (3, 0):
        finish(h)
    for g in range(groups):
        wait_bytes(y_in.at[g, pl.ds(0, ny - 1)], p_send.at[g])


def shards(nx, ny, nz, queries, keys, values, out_grad, doc_ids):
    part, width = queries.shape
    tok = part * nx
    heads = width // DH // nx
    group = min(GROUP, heads)
    groups = heads // group
    chips = nx // 2
    rows = DH // ny
    docs = doc_ids.reshape(-1, 128)
    operands = [
        pltpu.with_memory_space_constraint(x, pltpu.HBM)
        for x in (queries, keys, values, out_grad, docs)
    ]
    dma = pltpu.SemaphoreType.DMA
    results = pl.pallas_call(
        functools.partial(kernel, nx, ny, nz, heads, tok, group),
        out_shape=pltpu.VMEM((4, tok, heads * DH), BF16),
        in_specs=[pl.BlockSpec(memory_space=pltpu.HBM)] * 5,
        out_specs=pl.BlockSpec(memory_space=pltpu.VMEM),
        scratch_shapes=[
            pltpu.VMEM((4, chips, 2 * part, heads * DH), BF16),
            pltpu.VMEM((4, tok, heads * DH), BF16),
            pltpu.VMEM((4, heads, tok, DH), F32),
            pltpu.VMEM((tok, tok), BF16),
            pltpu.VMEM((tok, tok), BF16),
            pltpu.VMEM((4, tok, DH), BF16),
            pltpu.VMEM((ny * tok // 128, 128), jnp.int32),
            pltpu.SMEM((ny * tok // 128, 128), jnp.int32),
            pltpu.SMEM(docs.shape, jnp.int32),
            pltpu.SMEM((4, max(ny, nz)), F32),
            pltpu.VMEM((groups, chips, group, 2, DH, DH), BF16),
            pltpu.VMEM((groups, 2, group, 2, DH, DH), BF16),
            pltpu.VMEM((groups, 2, group, DH, DH), BF16),
            pltpu.VMEM((groups, 2, group, DH, DH), BF16),
            pltpu.VMEM((groups, group, 2, DH, DH), BF16),
            pltpu.VMEM((groups, ny, group, 2, rows, DH), BF16),
            pltpu.VMEM((groups, 2, group, rows, DH), BF16),
            pltpu.VMEM((groups, nz, group, rows, DH), BF16),
            pltpu.VMEM((groups, ny, group, 2, rows, DH), BF16),
            pltpu.VMEM((groups, group, 2, DH, DH), BF16),
            dma((3,)),
            dma((groups,)),
            dma((groups,)),
            dma((groups,)),
            dma((groups,)),
            dma((groups,)),
            dma((groups,)),
            dma((groups,)),
            pltpu.SemaphoreType.REGULAR,
            pltpu.SemaphoreType.REGULAR,
            dma((heads,)),
            dma((heads,)),
            dma((heads + 1,)),
            dma((groups,)),
            dma((groups,)),
            dma((groups,)),
            dma((groups,)),
            dma((groups,)),
            dma((groups,)),
        ],
        compiler_params=pltpu.CompilerParams(
            collective_id=0, has_side_effects=True, vmem_limit_bytes=40 * 1024 * 1024
        ),
    )(*operands)
    return tuple(results[i] for i in range(4))


def solution(mesh):
    nx, blocks = mesh.shape["head"], mesh.shape["ctx"]
    ny = min(ROW, blocks)
    rows = P(("ctx", "head"), None)
    return jax.shard_map(
        functools.partial(shards, nx, ny, blocks // ny),
        mesh=mesh,
        in_specs=(rows, rows, rows, rows, P()),
        out_specs=(P("ctx", "head"),) * 4,
        check_vma=False,
    )
```

```python
import functools

import jax
import jax.numpy as jnp
from jax import lax
from jax.experimental import pallas as pl
from jax.experimental.pallas import tpu as pltpu
from jax.sharding import PartitionSpec as P

DH = 128
ROW = 8
GROUP = 1
FIRST = 1
MESH = pl.DeviceIdType.MESH
F32, BF16 = jnp.float32, jnp.bfloat16
K, V, Q, G = range(4)
EARLY = (K,)


def nt(a, b):
    return lax.dot_general(a, b, (((1,), (1,)), ((), ())), preferred_element_type=F32)


def nn(a, b):
    return lax.dot_general(a, b, (((1,), (0,)), ((), ())), preferred_element_type=F32)


def tn(a, b):
    return lax.dot_general(a, b, (((0,), (0,)), ((), ())), preferred_element_type=F32)


def one_if(flag):
    return jnp.where(flag, F32(1.0), F32(0.0))


def far_first(count):
    return sorted(range(1, count), key=lambda step: -min(step, count - step))


def wait_bytes(ref, sem):
    if 0 not in ref.shape:
        pltpu.make_async_copy(ref, ref, sem).wait()


def kernel(
    nx, ny, nz, heads, tok, group,
    q_ref, k_ref, v_ref, g_ref, docs_ref,
    out_ref,
    pair, buf, acc, allow, allow_t, cols, docs_v, near_s, docs_s, keeps,
    part_out, part_in, relay_in, relay_out, st, y_in, z_out, z_in, p_out, held,
    docs_sem, own_sem, pair_send, pair_recv, part_send, part_recv, relay_send, relay_recv,
    line_in, cross_in, mine_sem, tok_send, tok_recv, y_send, y_recv, z_send, z_recv, p_send, p_recv,
):
    ctx = lax.axis_index("ctx")
    me_x = lax.axis_index("head")
    me_z, me_y = ctx // ny, ctx % ny
    chip, core = me_x // 2, me_x % 2
    chips = nx // 2
    groups = heads // group
    early = list(range(1, groups))
    turns = early + [0]
    part = tok // nx
    both = 2 * part
    rows = DH // ny
    per = tok // 128
    blocks = ny * nz
    wide = group * DH

    def chip_at(step):
        return lax.rem(chip + step, chips)

    def at_chip(step):
        return {"head": chip_at(step) * 2 + core}

    def y_peer(step):
        return lax.rem(me_y + step, ny)

    def at_y(step):
        return {"ctx": me_z * ny + y_peer(step)}

    def at_z(step):
        return {"ctx": lax.rem(me_z + step, nz) * ny + me_y}

    sibling = {"head": me_x + 1 - 2 * core}
    sources = (k_ref, v_ref, q_ref, g_ref)
    own_rows = pl.ds(pl.multiple_of(core * part, part), part)

    def columns(owner, first):
        return pl.ds(pl.multiple_of((owner * heads + first) * DH, DH), wide)

    row_docs = pl.ds(pl.multiple_of(me_z * ny * per, ny * per), ny * per)
    docs_copies = [
        pltpu.make_async_copy(docs_ref.at[row_docs], near_s, docs_sem.at[0]),
        pltpu.make_async_copy(docs_ref.at[row_docs], docs_v, docs_sem.at[1]),
        pltpu.make_async_copy(docs_ref, docs_s, docs_sem.at[2]),
    ]
    for copy in docs_copies:
        copy.start()
    for g in turns:
        for a in range(4):
            for c in range(chips):
                pltpu.make_async_copy(
                    sources[a].at[:, columns(c * 2 + core, g * group)],
                    pair.at[a, c, own_rows, pl.ds(g * wide, wide)],
                    own_sem.at[g],
                ).start()

    barrier = pltpu.get_barrier_semaphore()

    def greet(sem, peer):
        pl.semaphore_signal(sem, inc=1, device_id=peer, device_id_type=MESH)

    for step in range(1, chips):
        greet(barrier, {"head": lax.rem(chip + step, chips) * 2 + 1})
    pl.when(core == 0)(lambda: greet(barrier, sibling))
    across = [at_y(step) for step in range(1, ny)] + [at_z(step) for step in range(1, nz)]
    for peer in across:
        greet(barrier, {**peer, "head": chip * 2})

    @pl.when(core == 1)
    def _():
        pl.semaphore_wait(barrier, nx - 1)
        greet(line_in, sibling)

    @pl.when(core == 0)
    def _():
        pl.semaphore_wait(line_in, 1)

    for g in turns:
        for a in range(4):
            for c in range(chips):
                pltpu.make_async_remote_copy(
                    src_ref=sources[a].at[:, columns(c * 2 + 1 - core, g * group)],
                    dst_ref=pair.at[a, c, own_rows, pl.ds(g * wide, wide)],
                    send_sem=pair_send.at[g],
                    recv_sem=pair_recv.at[g],
                    device_id=sibling,
                    device_id_type=MESH,
                ).start()

    chip_rows = pl.ds(pl.multiple_of(chip * both, both), both)
    mine = pl.ds(pl.multiple_of(me_x * part, part), part)
    for a in EARLY:
        for step in range(1, chips):
            there = lax.rem(chip + step, chips) * 2
            for c in range(2):
                pltpu.make_async_remote_copy(
                    src_ref=sources[a].at[:, pl.ds(pl.multiple_of((there + c) * heads * DH, DH), DH)],
                    dst_ref=buf.at[a, mine, pl.ds(0, DH)],
                    send_sem=tok_send.at[0],
                    recv_sem=tok_recv.at[heads if a in (K, V) else 0],
                    device_id={"head": there + c},
                    device_id_type=MESH,
                ).start()

    for copy in docs_copies[:2]:
        copy.wait()

    def mark(n, doc):
        for i in range(per):
            cols[n, i * 128 : (i + 1) * 128, :] = one_if(col_of[i] == doc).astype(BF16)

    local = docs_v[pl.ds(pl.multiple_of(me_y * per, per), per), :]
    row_of = [jnp.broadcast_to(local[i : i + 1, :], (128, 128)) for i in range(per)]
    col_of = [r.T for r in row_of]
    mark(0, near_s[me_y * per + per - 1, 127])
    mark(1, near_s[me_y * per, 0])


    def wait_pair(g):
        half = pair.at[:, :, pl.ds(0, part), pl.ds(0, wide)]
        wait_bytes(half, own_sem.at[g])
        wait_bytes(half, pair_recv.at[g])

    def send_partials(g):
        wait_pair(g)
        tail, lead = cols[0, chip_rows, :], cols[1, chip_rows, :]
        for c in range(chips):
            for i in range(group):
                at = pl.ds((g * group + i) * DH, DH)
                part_out[g, c, i, 0] = tn(pair[K, c, :, at] * tail, pair[V, c, :, at]).astype(BF16)
                part_out[g, c, i, 1] = tn(pair[Q, c, :, at] * lead, pair[G, c, :, at]).astype(BF16)
        for n in range(2):
            near, far = (1, chips - 1) if n == 0 else (chips - 1, 1)
            pltpu.make_async_remote_copy(
                src_ref=part_out.at[g, chip_at(2), :, n],
                dst_ref=relay_in.at[g, n],
                send_sem=part_send.at[g],
                recv_sem=relay_recv.at[g],
                device_id=at_chip(near),
                device_id_type=MESH,
            ).start()
            pltpu.make_async_remote_copy(
                src_ref=part_out.at[g, chip_at(far), :, n],
                dst_ref=part_in.at[g, 0, :, n],
                send_sem=part_send.at[g],
                recv_sem=part_recv.at[g],
                device_id=at_chip(far),
                device_id_type=MESH,
            ).start()

    def relay_partials(g):
        wait_bytes(relay_in.at[g], relay_recv.at[g])
        for n in range(2):
            near = 1 if n == 0 else chips - 1
            relay_out[g, n] = (
                part_out[g, chip_at(near), :, n].astype(F32) + relay_in[g, n].astype(F32)
            ).astype(BF16)
            pltpu.make_async_remote_copy(
                src_ref=relay_out.at[g, n],
                dst_ref=part_in.at[g, 1, :, n],
                send_sem=relay_send.at[g],
                recv_sem=part_recv.at[g],
                device_id=at_chip(near),
                device_id_type=MESH,
            ).start()

    def send_tokens(h, arrays=range(4)):
        at = pl.ds(h * DH, DH)
        for a in arrays:
            for step in range(1, chips):
                pltpu.make_async_remote_copy(
                    src_ref=pair.at[a, chip_at(step), :, at],
                    dst_ref=buf.at[a, chip_rows, at],
                    send_sem=tok_send.at[h],
                    recv_sem=tok_recv.at[heads if h == 0 and a in (K, V) else h],
                    device_id=at_chip(step),
                    device_id_type=MESH,
                ).start()

    for g in early:
        send_partials(g)
    wait_pair(0)
    rest = [a for a in range(4) if a not in EARLY]
    send_tokens(0, rest[:FIRST])
    for g in early:
        relay_partials(g)
    send_tokens(0, rest[FIRST:])
    for h in range(1, heads):
        send_tokens(h)
    for h in range(heads):
        at = pl.ds(h * DH, DH)
        for a in range(4):
            pltpu.make_async_copy(
                pair.at[a, chip, :, at], buf.at[a, chip_rows, at], mine_sem.at[h]
            ).start()

    t_pos = lax.broadcasted_iota(jnp.int32, (128, 128), 0)
    s_pos = lax.broadcasted_iota(jnp.int32, (128, 128), 1)
    for i in range(per):
        at = slice(i * 128, (i + 1) * 128)
        for j in range(per):
            to = slice(j * 128, (j + 1) * 128)
            same = col_of[i] == row_of[j]
            allow[at, to] = one_if(same & (t_pos + i * 128 >= s_pos + j * 128)).astype(BF16)
            allow_t[at, to] = one_if(same & (t_pos + i * 128 <= s_pos + j * 128)).astype(BF16)

    docs_copies[2].wait()

    def last(block):
        return docs_s[block * per + per - 1, 127]

    def first(block):
        return docs_s[block * per, 0]

    mark(2, jnp.where(ctx == 0, -1, last(jnp.maximum(ctx - 1, 0))))
    mark(3, jnp.where(ctx == blocks - 1, -1, first(jnp.minimum(ctx + 1, blocks - 1))))

    base = me_z * ny
    before, after = last(jnp.maximum(base - 1, 0)), first(jnp.minimum(base + ny, blocks - 1))
    for y in range(ny):
        at = base + y
        keeps[0, y] = one_if(last(at) == last(jnp.maximum(at - 1, 0)))
        keeps[1, y] = one_if(first(at) == first(jnp.minimum(at + 1, blocks - 1)))
    for z in range(nz):
        keeps[2, z] = one_if((z < me_z) & (last(z * ny + ny - 1) == before))
        keeps[3, z] = one_if((z > me_z) & (first(z * ny) == after))

    def wait_tokens(h):
        wait_bytes(buf.at[:, pl.ds(0, both), pl.ds(0, DH)], mine_sem.at[h])
        wait_bytes(buf.at[:, pl.ds(0, tok - both), pl.ds(0, DH)], tok_recv.at[h])

    def stage_states(g):
        if g in early:
            wait_bytes(part_in.at[g], part_recv.at[g])
            for i in range(group):
                for n in range(2):
                    total = part_out[g, chip, i, n].astype(F32)
                    for c in range(2):
                        total = total + part_in[g, c, i, n].astype(F32)
                    st[g, i, n] = total.astype(BF16)
        else:
            for i in range(group):
                at = pl.ds((g * group + i) * DH, DH)
                wait_bytes(buf.at[:, pl.ds(0, both), pl.ds(0, DH)], mine_sem.at[0])
                wait_bytes(buf.at[pl.ds(0, 2), pl.ds(0, tok - both), pl.ds(0, DH)], tok_recv.at[heads])
                st[g, i, 0] = tn(buf[K, :, at] * cols[0], buf[V, :, at]).astype(BF16)
                wait_bytes(buf.at[pl.ds(0, 2), pl.ds(0, tok - both), pl.ds(0, DH)], tok_recv.at[0])
                st[g, i, 1] = tn(buf[Q, :, at] * cols[1], buf[G, :, at]).astype(BF16)
        for step in far_first(ny):
            slot = pl.multiple_of(y_peer(step) * rows, rows)
            pltpu.make_async_remote_copy(
                src_ref=st.at[g, :, :, pl.ds(slot, rows), :],
                dst_ref=y_in.at[g, me_y],
                send_sem=y_send.at[g],
                recv_sem=y_recv.at[g],
                device_id=at_y(step),
                device_id_type=MESH,
            ).start()
        y_in[g, me_y] = st[g, :, :, pl.ds(pl.multiple_of(me_y * rows, rows), rows), :]

    def stage_totals(g):
        wait_bytes(y_in.at[g, pl.ds(0, ny - 1)], y_recv.at[g])
        total = y_in[g, 0, :, 0].astype(F32)
        for y in range(1, ny):
            total = y_in[g, y, :, 0].astype(F32) + keeps[0, y] * total
        z_out[g, 0] = total.astype(BF16)
        total = y_in[g, ny - 1, :, 1].astype(F32)
        for y in reversed(range(ny - 1)):
            total = y_in[g, y, :, 1].astype(F32) + keeps[1, y] * total
        z_out[g, 1] = total.astype(BF16)
        for step in far_first(nz):
            pltpu.make_async_remote_copy(
                src_ref=z_out.at[g, (me_z + step) // nz],
                dst_ref=z_in.at[g, me_z],
                send_sem=z_send.at[g],
                recv_sem=z_recv.at[g],
                device_id=at_z(step),
                device_id_type=MESH,
            ).start()
        z_in[g, me_z] = jnp.zeros((group, rows, DH), BF16)

    def stage_prefix(g):
        wait_bytes(z_in.at[g, pl.ds(0, nz - 1)], z_recv.at[g])
        state = jnp.zeros((group, rows, DH), F32)
        gstate = jnp.zeros((group, rows, DH), F32)
        for z in range(nz):
            term = z_in[g, z].astype(F32)
            state = state + keeps[2, z] * term
            gstate = gstate + keeps[3, z] * term
        for y in range(ny):
            p_out[g, y, :, 0] = state.astype(BF16)
            if y < ny - 1:
                state = y_in[g, y, :, 0].astype(F32) + keeps[0, y] * state
        for y in reversed(range(ny)):
            p_out[g, y, :, 1] = gstate.astype(BF16)
            if y > 0:
                gstate = y_in[g, y, :, 1].astype(F32) + keeps[1, y] * gstate
        here = pl.ds(pl.multiple_of(me_y * rows, rows), rows)
        for step in far_first(ny):
            pltpu.make_async_remote_copy(
                src_ref=p_out.at[g, y_peer(step)],
                dst_ref=held.at[g, :, :, here, :],
                send_sem=p_send.at[g],
                recv_sem=p_recv.at[g],
                device_id=at_y(step),
                device_id_type=MESH,
            ).start()
        held[g, :, :, here, :] = p_out[g, me_y]

    tile = min(256, tok)

    def scores(h, left, right, by_row, by_col):
        here = pl.ds(pl.multiple_of(h * DH, DH), DH)
        for i in range(tok // tile):
            at, upto = slice(i * tile, (i + 1) * tile), slice(0, (i + 1) * tile)
            s = nt(buf[left, at, here], buf[right, upto, here]).astype(BF16) * allow[at, upto]
            acc[by_row[0], h, at, :] = nn(s, buf[by_row[1], upto, here])
            onward = slice(i * tile, tok)
            s = nt(buf[right, at, here], buf[left, onward, here]).astype(BF16) * allow_t[at, onward]
            acc[by_col[0], h, at, :] = nn(s, buf[by_col[1], onward, here])

    def intra(h, carry):
        pl.when(h >= group)(lambda: wait_tokens(h))
        scores(h, Q, K, (0, V), (3, G))
        scores(h, G, V, (1, K), (2, Q))
        return carry

    def finish(h):
        g, i = h // group, h % group
        if i == 0:
            wait_bytes(y_in.at[g, pl.ds(0, ny - 1)], p_recv.at[g])
        here = pl.ds(h * DH, DH)
        state, gstate = held[g, i, 0], held[g, i, 1]
        match, back = cols[2], cols[3]
        out_ref[0, :, here] = (acc[0, h] + nn(buf[Q, :, here] * match, state)).astype(BF16)
        out_ref[1, :, here] = (acc[1, h] + nt(buf[G, :, here] * match, state)).astype(BF16)
        out_ref[2, :, here] = (acc[2, h] + nt(buf[V, :, here] * back, gstate)).astype(BF16)
        out_ref[3, :, here] = (acc[3, h] + nn(buf[K, :, here] * back, gstate)).astype(BF16)

    @pl.when(core == 0)
    def _():
        pl.semaphore_wait(barrier, 2 * len(across))
        greet(cross_in, sibling)

    @pl.when(core == 1)
    def _():
        pl.semaphore_wait(cross_in, 1)

    for g in early:
        stage_states(g)
    stage_totals(early[0])
    stage_states(0)
    for g in early[1:] + [0]:
        stage_totals(g)
    lax.fori_loop(0, 2, intra, 0)
    for g in turns:
        stage_prefix(g)
    lax.fori_loop(2, 3, intra, 0)
    for h in (1, 2):
        finish(h)
    lax.fori_loop(3, 4, intra, 0)
    for g in range(groups):
        wait_bytes(pair.at[:, :, pl.ds(0, part), pl.ds(0, wide)], pair_send.at[g])
        if g in early:
            wait_bytes(part_in.at[g], part_send.at[g])
            wait_bytes(relay_in.at[g], relay_send.at[g])
        wait_bytes(y_in.at[g, pl.ds(0, ny - 1)], y_send.at[g])
        wait_bytes(z_in.at[g, pl.ds(0, nz - 1)], z_send.at[g])
    for h in range(heads):
        wait_bytes(buf.at[:, pl.ds(0, tok - both), pl.ds(0, DH)], tok_send.at[h])
    for h in (3, 0):
        finish(h)
    for g in range(groups):
        wait_bytes(y_in.at[g, pl.ds(0, ny - 1)], p_send.at[g])


def shards(nx, ny, nz, queries, keys, values, out_grad, doc_ids):
    part, width = queries.shape
    tok = part * nx
    heads = width // DH // nx
    group = min(GROUP, heads)
    groups = heads // group
    chips = nx // 2
    rows = DH // ny
    docs = doc_ids.reshape(-1, 128)
    operands = [
        pltpu.with_memory_space_constraint(x, pltpu.HBM)
        for x in (queries, keys, values, out_grad, docs)
    ]
    dma = pltpu.SemaphoreType.DMA
    results = pl.pallas_call(
        functools.partial(kernel, nx, ny, nz, heads, tok, group),
        out_shape=pltpu.VMEM((4, tok, heads * DH), BF16),
        in_specs=[pl.BlockSpec(memory_space=pltpu.HBM)] * 5,
        out_specs=pl.BlockSpec(memory_space=pltpu.VMEM),
        scratch_shapes=[
            pltpu.VMEM((4, chips, 2 * part, heads * DH), BF16),
            pltpu.VMEM((4, tok, heads * DH), BF16),
            pltpu.VMEM((4, heads, tok, DH), F32),
            pltpu.VMEM((tok, tok), BF16),
            pltpu.VMEM((tok, tok), BF16),
            pltpu.VMEM((4, tok, DH), BF16),
            pltpu.VMEM((ny * tok // 128, 128), jnp.int32),
            pltpu.SMEM((ny * tok // 128, 128), jnp.int32),
            pltpu.SMEM(docs.shape, jnp.int32),
            pltpu.SMEM((4, max(ny, nz)), F32),
            pltpu.VMEM((groups, chips, group, 2, DH, DH), BF16),
            pltpu.VMEM((groups, 2, group, 2, DH, DH), BF16),
            pltpu.VMEM((groups, 2, group, DH, DH), BF16),
            pltpu.VMEM((groups, 2, group, DH, DH), BF16),
            pltpu.VMEM((groups, group, 2, DH, DH), BF16),
            pltpu.VMEM((groups, ny, group, 2, rows, DH), BF16),
            pltpu.VMEM((groups, 2, group, rows, DH), BF16),
            pltpu.VMEM((groups, nz, group, rows, DH), BF16),
            pltpu.VMEM((groups, ny, group, 2, rows, DH), BF16),
            pltpu.VMEM((groups, group, 2, DH, DH), BF16),
            dma((3,)),
            dma((groups,)),
            dma((groups,)),
            dma((groups,)),
            dma((groups,)),
            dma((groups,)),
            dma((groups,)),
            dma((groups,)),
            pltpu.SemaphoreType.REGULAR,
            pltpu.SemaphoreType.REGULAR,
            dma((heads,)),
            dma((heads,)),
            dma((heads + 1,)),
            dma((groups,)),
            dma((groups,)),
            dma((groups,)),
            dma((groups,)),
            dma((groups,)),
            dma((groups,)),
        ],
        compiler_params=pltpu.CompilerParams(
            collective_id=0, has_side_effects=True, vmem_limit_bytes=40 * 1024 * 1024
        ),
    )(*operands)
    return tuple(results[i] for i in range(4))


def solution(mesh):
    nx, blocks = mesh.shape["head"], mesh.shape["ctx"]
    ny = min(ROW, blocks)
    rows = P(("ctx", "head"), None)
    return jax.shard_map(
        functools.partial(shards, nx, ny, blocks // ny),
        mesh=mesh,
        in_specs=(rows, rows, rows, rows, P()),
        out_specs=(P("ctx", "head"),) * 4,
        check_vma=False,
    )
```

```python
import functools

import jax
import jax.numpy as jnp
from jax import lax
from jax.experimental import pallas as pl
from jax.experimental.pallas import tpu as pltpu
from jax.sharding import PartitionSpec as P

DH = 128
ROW = 8
GROUP = 1
FIRST = 1
MESH = pl.DeviceIdType.MESH
F32, BF16 = jnp.float32, jnp.bfloat16
K, V, Q, G = range(4)
EARLY = (K,)


def nt(a, b):
    return lax.dot_general(a, b, (((1,), (1,)), ((), ())), preferred_element_type=F32)


def nn(a, b):
    return lax.dot_general(a, b, (((1,), (0,)), ((), ())), preferred_element_type=F32)


def tn(a, b):
    return lax.dot_general(a, b, (((0,), (0,)), ((), ())), preferred_element_type=F32)


def one_if(flag):
    return jnp.where(flag, F32(1.0), F32(0.0))


def far_first(count):
    return sorted(range(1, count), key=lambda step: -min(step, count - step))


def wait_bytes(ref, sem):
    if 0 not in ref.shape:
        pltpu.make_async_copy(ref, ref, sem).wait()


def kernel(
    nx, ny, nz, heads, tok, group,
    q_ref, k_ref, v_ref, g_ref, docs_ref,
    out_ref,
    pair, buf, acc, allow, allow_t, cols, docs_v, near_s, docs_s, keeps,
    part_out, part_in, relay_in, relay_out, st, y_in, z_out, z_in, p_out, held,
    docs_sem, own_sem, pair_send, pair_recv, part_send, part_recv, relay_send, relay_recv,
    line_in, cross_in, mine_sem, tok_send, tok_recv, y_send, y_recv, z_send, z_recv, p_send, p_recv,
):
    ctx = lax.axis_index("ctx")
    me_x = lax.axis_index("head")
    me_z, me_y = ctx // ny, ctx % ny
    chip, core = me_x // 2, me_x % 2
    chips = nx // 2
    groups = heads // group
    early = list(range(1, groups))
    turns = early + [0]
    part = tok // nx
    both = 2 * part
    rows = DH // ny
    per = tok // 128
    blocks = ny * nz
    wide = group * DH

    def chip_at(step):
        return lax.rem(chip + step, chips)

    def at_chip(step):
        return {"head": chip_at(step) * 2 + core}

    def y_peer(step):
        return lax.rem(me_y + step, ny)

    def at_y(step):
        return {"ctx": me_z * ny + y_peer(step)}

    def at_z(step):
        return {"ctx": lax.rem(me_z + step, nz) * ny + me_y}

    sibling = {"head": me_x + 1 - 2 * core}
    sources = (k_ref, v_ref, q_ref, g_ref)
    own_rows = pl.ds(pl.multiple_of(core * part, part), part)

    def columns(owner, first):
        return pl.ds(pl.multiple_of((owner * heads + first) * DH, DH), wide)

    row_docs = pl.ds(pl.multiple_of(me_z * ny * per, ny * per), ny * per)
    docs_copies = [
        pltpu.make_async_copy(docs_ref.at[row_docs], near_s, docs_sem.at[0]),
        pltpu.make_async_copy(docs_ref.at[row_docs], docs_v, docs_sem.at[1]),
        pltpu.make_async_copy(docs_ref, docs_s, docs_sem.at[2]),
    ]
    for copy in docs_copies:
        copy.start()
    for g in turns:
        for a in range(4):
            for c in range(chips):
                pltpu.make_async_copy(
                    sources[a].at[:, columns(c * 2 + core, g * group)],
                    pair.at[a, c, own_rows, pl.ds(g * wide, wide)],
                    own_sem.at[g],
                ).start()

    barrier = pltpu.get_barrier_semaphore()

    def greet(sem, peer):
        pl.semaphore_signal(sem, inc=1, device_id=peer, device_id_type=MESH)

    for step in range(1, chips):
        greet(barrier, {"head": lax.rem(chip + step, chips) * 2 + 1})
    pl.when(core == 0)(lambda: greet(barrier, sibling))
    across = [at_y(step) for step in range(1, ny)] + [at_z(step) for step in range(1, nz)]
    for peer in across:
        greet(barrier, {**peer, "head": chip * 2})

    @pl.when(core == 1)
    def _():
        pl.semaphore_wait(barrier, nx - 1)
        greet(line_in, sibling)

    @pl.when(core == 0)
    def _():
        pl.semaphore_wait(line_in, 1)

    for g in turns:
        for a in range(4):
            for c in range(chips):
                pltpu.make_async_remote_copy(
                    src_ref=sources[a].at[:, columns(c * 2 + 1 - core, g * group)],
                    dst_ref=pair.at[a, c, own_rows, pl.ds(g * wide, wide)],
                    send_sem=pair_send.at[g],
                    recv_sem=pair_recv.at[g],
                    device_id=sibling,
                    device_id_type=MESH,
                ).start()

    chip_rows = pl.ds(pl.multiple_of(chip * both, both), both)
    mine = pl.ds(pl.multiple_of(me_x * part, part), part)
    for a in EARLY:
        for step in range(1, chips):
            there = lax.rem(chip + step, chips) * 2
            for c in range(2):
                pltpu.make_async_remote_copy(
                    src_ref=sources[a].at[:, pl.ds(pl.multiple_of((there + c) * heads * DH, DH), DH)],
                    dst_ref=buf.at[a, mine, pl.ds(0, DH)],
                    send_sem=tok_send.at[0],
                    recv_sem=tok_recv.at[heads if a in (K, V) else 0],
                    device_id={"head": there + c},
                    device_id_type=MESH,
                ).start()

    for copy in docs_copies[:2]:
        copy.wait()

    def mark(n, doc):
        for i in range(per):
            cols[n, i * 128 : (i + 1) * 128, :] = one_if(col_of[i] == doc).astype(BF16)

    local = docs_v[pl.ds(pl.multiple_of(me_y * per, per), per), :]
    row_of = [jnp.broadcast_to(local[i : i + 1, :], (128, 128)) for i in range(per)]
    col_of = [r.T for r in row_of]
    mark(0, near_s[me_y * per + per - 1, 127])
    mark(1, near_s[me_y * per, 0])


    def wait_pair(g):
        half = pair.at[:, :, pl.ds(0, part), pl.ds(0, wide)]
        wait_bytes(half, own_sem.at[g])
        wait_bytes(half, pair_recv.at[g])

    def send_partials(g):
        wait_pair(g)
        tail, lead = cols[0, chip_rows, :], cols[1, chip_rows, :]
        for c in range(chips):
            for i in range(group):
                at = pl.ds((g * group + i) * DH, DH)
                part_out[g, c, i, 0] = tn(pair[K, c, :, at] * tail, pair[V, c, :, at]).astype(BF16)
                part_out[g, c, i, 1] = tn(pair[Q, c, :, at] * lead, pair[G, c, :, at]).astype(BF16)
        for n in range(2):
            near, far = (1, chips - 1) if n == 0 else (chips - 1, 1)
            pltpu.make_async_remote_copy(
                src_ref=part_out.at[g, chip_at(2), :, n],
                dst_ref=relay_in.at[g, n],
                send_sem=part_send.at[g],
                recv_sem=relay_recv.at[g],
                device_id=at_chip(near),
                device_id_type=MESH,
            ).start()
            pltpu.make_async_remote_copy(
                src_ref=part_out.at[g, chip_at(far), :, n],
                dst_ref=part_in.at[g, 0, :, n],
                send_sem=part_send.at[g],
                recv_sem=part_recv.at[g],
                device_id=at_chip(far),
                device_id_type=MESH,
            ).start()

    def relay_partials(g):
        wait_bytes(relay_in.at[g], relay_recv.at[g])
        for n in range(2):
            near = 1 if n == 0 else chips - 1
            relay_out[g, n] = (
                part_out[g, chip_at(near), :, n].astype(F32) + relay_in[g, n].astype(F32)
            ).astype(BF16)
            pltpu.make_async_remote_copy(
                src_ref=relay_out.at[g, n],
                dst_ref=part_in.at[g, 1, :, n],
                send_sem=relay_send.at[g],
                recv_sem=part_recv.at[g],
                device_id=at_chip(near),
                device_id_type=MESH,
            ).start()

    def send_tokens(h, arrays=range(4)):
        at = pl.ds(h * DH, DH)
        for a in arrays:
            for step in range(1, chips):
                pltpu.make_async_remote_copy(
                    src_ref=pair.at[a, chip_at(step), :, at],
                    dst_ref=buf.at[a, chip_rows, at],
                    send_sem=tok_send.at[h],
                    recv_sem=tok_recv.at[heads + h if a in ((K, V) if h == 0 else (G,)) else h],
                    device_id=at_chip(step),
                    device_id_type=MESH,
                ).start()

    for g in early:
        send_partials(g)
    wait_pair(0)
    rest = [a for a in range(4) if a not in EARLY]
    send_tokens(0, rest[:FIRST])
    for g in early:
        relay_partials(g)
    send_tokens(0, rest[FIRST:])
    for h in range(1, heads):
        send_tokens(h)
    for h in range(heads):
        at = pl.ds(h * DH, DH)
        for a in range(4):
            pltpu.make_async_copy(
                pair.at[a, chip, :, at], buf.at[a, chip_rows, at], mine_sem.at[h]
            ).start()

    t_pos = lax.broadcasted_iota(jnp.int32, (128, 128), 0)
    s_pos = lax.broadcasted_iota(jnp.int32, (128, 128), 1)
    for i in range(per):
        at = slice(i * 128, (i + 1) * 128)
        for j in range(per):
            to = slice(j * 128, (j + 1) * 128)
            same = col_of[i] == row_of[j]
            allow[at, to] = one_if(same & (t_pos + i * 128 >= s_pos + j * 128)).astype(BF16)
            allow_t[at, to] = one_if(same & (t_pos + i * 128 <= s_pos + j * 128)).astype(BF16)

    docs_copies[2].wait()

    def last(block):
        return docs_s[block * per + per - 1, 127]

    def first(block):
        return docs_s[block * per, 0]

    mark(2, jnp.where(ctx == 0, -1, last(jnp.maximum(ctx - 1, 0))))
    mark(3, jnp.where(ctx == blocks - 1, -1, first(jnp.minimum(ctx + 1, blocks - 1))))

    base = me_z * ny
    before, after = last(jnp.maximum(base - 1, 0)), first(jnp.minimum(base + ny, blocks - 1))
    for y in range(ny):
        at = base + y
        keeps[0, y] = one_if(last(at) == last(jnp.maximum(at - 1, 0)))
        keeps[1, y] = one_if(first(at) == first(jnp.minimum(at + 1, blocks - 1)))
    for z in range(nz):
        keeps[2, z] = one_if((z < me_z) & (last(z * ny + ny - 1) == before))
        keeps[3, z] = one_if((z > me_z) & (first(z * ny) == after))

    def stage_states(g):
        if g in early:
            wait_bytes(part_in.at[g], part_recv.at[g])
            for i in range(group):
                for n in range(2):
                    total = part_out[g, chip, i, n].astype(F32)
                    for c in range(2):
                        total = total + part_in[g, c, i, n].astype(F32)
                    st[g, i, n] = total.astype(BF16)
        else:
            for i in range(group):
                at = pl.ds((g * group + i) * DH, DH)
                wait_bytes(buf.at[:, pl.ds(0, both), pl.ds(0, DH)], mine_sem.at[0])
                wait_bytes(buf.at[pl.ds(0, 2), pl.ds(0, tok - both), pl.ds(0, DH)], tok_recv.at[heads])
                st[g, i, 0] = tn(buf[K, :, at] * cols[0], buf[V, :, at]).astype(BF16)
                wait_bytes(buf.at[pl.ds(0, 2), pl.ds(0, tok - both), pl.ds(0, DH)], tok_recv.at[0])
                st[g, i, 1] = tn(buf[Q, :, at] * cols[1], buf[G, :, at]).astype(BF16)
        for step in far_first(ny):
            slot = pl.multiple_of(y_peer(step) * rows, rows)
            pltpu.make_async_remote_copy(
                src_ref=st.at[g, :, :, pl.ds(slot, rows), :],
                dst_ref=y_in.at[g, me_y],
                send_sem=y_send.at[g],
                recv_sem=y_recv.at[g],
                device_id=at_y(step),
                device_id_type=MESH,
            ).start()
        y_in[g, me_y] = st[g, :, :, pl.ds(pl.multiple_of(me_y * rows, rows), rows), :]

    def stage_totals(g):
        wait_bytes(y_in.at[g, pl.ds(0, ny - 1)], y_recv.at[g])
        total = y_in[g, 0, :, 0].astype(F32)
        for y in range(1, ny):
            total = y_in[g, y, :, 0].astype(F32) + keeps[0, y] * total
        z_out[g, 0] = total.astype(BF16)
        total = y_in[g, ny - 1, :, 1].astype(F32)
        for y in reversed(range(ny - 1)):
            total = y_in[g, y, :, 1].astype(F32) + keeps[1, y] * total
        z_out[g, 1] = total.astype(BF16)
        for step in far_first(nz):
            pltpu.make_async_remote_copy(
                src_ref=z_out.at[g, (me_z + step) // nz],
                dst_ref=z_in.at[g, me_z],
                send_sem=z_send.at[g],
                recv_sem=z_recv.at[g],
                device_id=at_z(step),
                device_id_type=MESH,
            ).start()
        z_in[g, me_z] = jnp.zeros((group, rows, DH), BF16)

    def stage_prefix(g):
        wait_bytes(z_in.at[g, pl.ds(0, nz - 1)], z_recv.at[g])
        state = jnp.zeros((group, rows, DH), F32)
        gstate = jnp.zeros((group, rows, DH), F32)
        for z in range(nz):
            term = z_in[g, z].astype(F32)
            state = state + keeps[2, z] * term
            gstate = gstate + keeps[3, z] * term
        for y in range(ny):
            p_out[g, y, :, 0] = state.astype(BF16)
            if y < ny - 1:
                state = y_in[g, y, :, 0].astype(F32) + keeps[0, y] * state
        for y in reversed(range(ny)):
            p_out[g, y, :, 1] = gstate.astype(BF16)
            if y > 0:
                gstate = y_in[g, y, :, 1].astype(F32) + keeps[1, y] * gstate
        here = pl.ds(pl.multiple_of(me_y * rows, rows), rows)
        for step in far_first(ny):
            pltpu.make_async_remote_copy(
                src_ref=p_out.at[g, y_peer(step)],
                dst_ref=held.at[g, :, :, here, :],
                send_sem=p_send.at[g],
                recv_sem=p_recv.at[g],
                device_id=at_y(step),
                device_id_type=MESH,
            ).start()
        held[g, :, :, here, :] = p_out[g, me_y]

    tile = min(256, tok)

    def by_rows(h, left, right, to, by):
        here = pl.ds(pl.multiple_of(h * DH, DH), DH)
        for i in range(tok // tile):
            at, upto = slice(i * tile, (i + 1) * tile), slice(0, (i + 1) * tile)
            s = nt(buf[left, at, here], buf[right, upto, here]).astype(BF16) * allow[at, upto]
            acc[to, h, at, :] = nn(s, buf[by, upto, here])

    def by_columns(h, left, right, to, by):
        here = pl.ds(pl.multiple_of(h * DH, DH), DH)
        for i in range(tok // tile):
            at, onward = slice(i * tile, (i + 1) * tile), slice(i * tile, tok)
            s = nt(buf[right, at, here], buf[left, onward, here]).astype(BF16) * allow_t[at, onward]
            acc[to, h, at, :] = nn(s, buf[by, onward, here])

    def intra(h, carry):
        @pl.when(h >= group)
        def _():
            wait_bytes(buf.at[:, pl.ds(0, both), pl.ds(0, DH)], mine_sem.at[h])
            wait_bytes(buf.at[pl.ds(0, 3), pl.ds(0, tok - both), pl.ds(0, DH)], tok_recv.at[h])

        by_rows(h, Q, K, 0, V)
        pl.when(h >= group)(
            lambda: wait_bytes(buf.at[G, pl.ds(0, tok - both), pl.ds(0, DH)], tok_recv.at[heads + h])
        )
        by_columns(h, Q, K, 3, G)
        by_rows(h, G, V, 1, K)
        by_columns(h, G, V, 2, Q)
        return carry

    def finish(h):
        g, i = h // group, h % group
        if i == 0:
            wait_bytes(y_in.at[g, pl.ds(0, ny - 1)], p_recv.at[g])
        here = pl.ds(h * DH, DH)
        state, gstate = held[g, i, 0], held[g, i, 1]
        match, back = cols[2], cols[3]
        out_ref[0, :, here] = (acc[0, h] + nn(buf[Q, :, here] * match, state)).astype(BF16)
        out_ref[1, :, here] = (acc[1, h] + nt(buf[G, :, here] * match, state)).astype(BF16)
        out_ref[2, :, here] = (acc[2, h] + nt(buf[V, :, here] * back, gstate)).astype(BF16)
        out_ref[3, :, here] = (acc[3, h] + nn(buf[K, :, here] * back, gstate)).astype(BF16)

    @pl.when(core == 0)
    def _():
        pl.semaphore_wait(barrier, 2 * len(across))
        greet(cross_in, sibling)

    @pl.when(core == 1)
    def _():
        pl.semaphore_wait(cross_in, 1)

    for g in early:
        stage_states(g)
    stage_totals(early[0])
    stage_states(0)
    for g in early[1:] + [0]:
        stage_totals(g)
    lax.fori_loop(0, 2, intra, 0)
    for g in turns:
        stage_prefix(g)
    lax.fori_loop(2, 3, intra, 0)
    for h in (1, 2):
        finish(h)
    lax.fori_loop(3, 4, intra, 0)
    for g in range(groups):
        wait_bytes(pair.at[:, :, pl.ds(0, part), pl.ds(0, wide)], pair_send.at[g])
        if g in early:
            wait_bytes(part_in.at[g], part_send.at[g])
            wait_bytes(relay_in.at[g], relay_send.at[g])
        wait_bytes(y_in.at[g, pl.ds(0, ny - 1)], y_send.at[g])
        wait_bytes(z_in.at[g, pl.ds(0, nz - 1)], z_send.at[g])
    for h in range(heads):
        wait_bytes(buf.at[:, pl.ds(0, tok - both), pl.ds(0, DH)], tok_send.at[h])
    for h in (3, 0):
        finish(h)
    for g in range(groups):
        wait_bytes(y_in.at[g, pl.ds(0, ny - 1)], p_send.at[g])


def shards(nx, ny, nz, queries, keys, values, out_grad, doc_ids):
    part, width = queries.shape
    tok = part * nx
    heads = width // DH // nx
    group = min(GROUP, heads)
    groups = heads // group
    chips = nx // 2
    rows = DH // ny
    docs = doc_ids.reshape(-1, 128)
    operands = [
        pltpu.with_memory_space_constraint(x, pltpu.HBM)
        for x in (queries, keys, values, out_grad, docs)
    ]
    dma = pltpu.SemaphoreType.DMA
    results = pl.pallas_call(
        functools.partial(kernel, nx, ny, nz, heads, tok, group),
        out_shape=pltpu.VMEM((4, tok, heads * DH), BF16),
        in_specs=[pl.BlockSpec(memory_space=pltpu.HBM)] * 5,
        out_specs=pl.BlockSpec(memory_space=pltpu.VMEM),
        scratch_shapes=[
            pltpu.VMEM((4, chips, 2 * part, heads * DH), BF16),
            pltpu.VMEM((4, tok, heads * DH), BF16),
            pltpu.VMEM((4, heads, tok, DH), F32),
            pltpu.VMEM((tok, tok), BF16),
            pltpu.VMEM((tok, tok), BF16),
            pltpu.VMEM((4, tok, DH), BF16),
            pltpu.VMEM((ny * tok // 128, 128), jnp.int32),
            pltpu.SMEM((ny * tok // 128, 128), jnp.int32),
            pltpu.SMEM(docs.shape, jnp.int32),
            pltpu.SMEM((4, max(ny, nz)), F32),
            pltpu.VMEM((groups, chips, group, 2, DH, DH), BF16),
            pltpu.VMEM((groups, 2, group, 2, DH, DH), BF16),
            pltpu.VMEM((groups, 2, group, DH, DH), BF16),
            pltpu.VMEM((groups, 2, group, DH, DH), BF16),
            pltpu.VMEM((groups, group, 2, DH, DH), BF16),
            pltpu.VMEM((groups, ny, group, 2, rows, DH), BF16),
            pltpu.VMEM((groups, 2, group, rows, DH), BF16),
            pltpu.VMEM((groups, nz, group, rows, DH), BF16),
            pltpu.VMEM((groups, ny, group, 2, rows, DH), BF16),
            pltpu.VMEM((groups, group, 2, DH, DH), BF16),
            dma((3,)),
            dma((groups,)),
            dma((groups,)),
            dma((groups,)),
            dma((groups,)),
            dma((groups,)),
            dma((groups,)),
            dma((groups,)),
            pltpu.SemaphoreType.REGULAR,
            pltpu.SemaphoreType.REGULAR,
            dma((heads,)),
            dma((heads,)),
            dma((2 * heads,)),
            dma((groups,)),
            dma((groups,)),
            dma((groups,)),
            dma((groups,)),
            dma((groups,)),
            dma((groups,)),
        ],
        compiler_params=pltpu.CompilerParams(
            collective_id=0, has_side_effects=True, vmem_limit_bytes=40 * 1024 * 1024
        ),
    )(*operands)
    return tuple(results[i] for i in range(4))


def solution(mesh):
    nx, blocks = mesh.shape["head"], mesh.shape["ctx"]
    ny = min(ROW, blocks)
    rows = P(("ctx", "head"), None)
    return jax.shard_map(
        functools.partial(shards, nx, ny, blocks // ny),
        mesh=mesh,
        in_specs=(rows, rows, rows, rows, P()),
        out_specs=(P("ctx", "head"),) * 4,
        check_vma=False,
    )
```
